32 devices in a mesh: groups: 2 (over y), scan: 4 (over x, core), tile: 4 (over z).
Axes of the slice: x: 2, y: 2, z: 4, core: 2. Of those that a mesh axis runs over, the one named last changes fastest.
Arguments:
- object_field: float32 [2, 1024, 2048], P(None, ('groups', 'scan'), 'tile'), parts along dimension 1, may hold values from -5 to 5
- probe: float32 [16, 2, 256, 256], P('groups'), parts along dimension 0, may hold values from -1.5 to 1.5
- measured: float32 [32, 256, 256], P(('groups', 'scan', 'tile')), parts along dimension 0, may hold values from 0 to 1
- positions: int32 [32, 2], P('groups'), parts along dimension 0, may hold values from 0 to 1792, as said below
Outputs:
- object_gradient: float32 [2, 1024, 2048], P(None, ('groups', 'scan'), 'tile'), parts along dimension 1
- probe_gradient: float32 [16, 2, 256, 256], P(('groups', 'tile')), parts along dimension 0
The draws below stay inside these ranges and needn't reach their ends.
There are 2 independent parts, one for each index of `groups`. The reference program is written for one: setup_inputs(seed, part) draws one part's arguments, and reference() takes and returns one part's arrays. A program takes and returns all parts, laid end to end along the dimension named above; each array names one. Nothing has to cross between parts.
Inputs may be any that keep to these rules, and one draw needn't show every extreme that they name: `positions`: each row lies in 0 to 256 and each column in 0 to 1792, so every patch lies inside the object; some patch touches the top, the bottom and the right edge.
All inputs are finite; a program needn't handle non-finite values.
Results may differ from the reference program's by a relative error of at most 0.0003.
Values sent between devices are 32-bit elements; how exact they have to be, the bound alone decides.
A program may use at most 128 MiB of HBM per device.

```python
import jax
import jax.numpy as jnp
from jax import lax

W = 256
MODES = 8
ROWS = 512
COLS = 2048
POSITIONS = 16


def draw_positions(key, part):
    row_key = jax.random.fold_in(key, 11)
    col_key = jax.random.fold_in(key, 12)
    row_vals = jax.random.randint(row_key, (POSITIONS,), 0, ROWS - W + 1)
    col_vals = jax.random.randint(col_key, (POSITIONS,), 0, COLS - W + 1)
    row_vals = row_vals.at[0].set(0).at[1].set(ROWS - W)
    col_vals = col_vals.at[0].set(0).at[2].set(COLS - W)
    return jnp.stack([row_vals, col_vals], axis=1).astype(jnp.int32)


def block_scale(rng, extent, cuts, smallest, top_value):
    level = 1.0
    for dim, shards_of in cuts:
        heights = jax.random.uniform(jax.random.fold_in(jax.random.fold_in(rng, 6), dim), (shards_of,), jnp.float32, smallest / len(cuts), top_value / len(cuts))
        level = level * jnp.repeat(jnp.exp(heights), extent[dim] // shards_of).reshape((-1,) + (1,) * (len(extent) - 1 - dim))
    return level


def scatter_about(stream_key, shape, scale, bound, pieces=(), kind=jnp.bfloat16):
    result = jax.random.normal(stream_key, shape, jnp.float32) * scale
    if len(pieces) > 0:
        result = block_scale(stream_key, shape, pieces, -0.22, 0.18) * result
    return jnp.clip(result, min=-bound, max=bound).astype(kind)


def setup_inputs(seed: int = 0, part: int = 0) -> dict:
    key_of = jax.random.split(jax.random.key(seed), 5)
    own_keys = jax.random.split(jax.random.fold_in(key_of[4], part), 5)
    object_field = scatter_about(own_keys[0], (2, ROWS, COLS), 0.7, 5.0, ((1, 4), (2, 4)), jnp.float32)
    probe = scatter_about(own_keys[1], (MODES, 2, W, W), 0.25, 1.5, (), jnp.float32)
    measured = jnp.clip(1.0 * jax.random.uniform(own_keys[2], (POSITIONS, W, W), jnp.float32) ** block_scale(own_keys[2], (POSITIONS, W, W), ((0, 16),), -0.2, 0.2), 0.0, 1.0)
    positions = draw_positions(jax.random.fold_in(jax.random.fold_in(key_of[4], part), 71), part)
    return dict(object_field=object_field, probe=probe, measured=measured, positions=positions)


def reference(object_field, probe, measured, positions):
    probe_cplx = lax.complex(probe[:, 0], probe[:, 1])
    probe_power = jnp.sum(probe[:, 0] * probe[:, 0] + probe[:, 1] * probe[:, 1], axis=0)
    anchor = jnp.zeros((), jnp.int32)

    def visit(carry, item):
        object_acc, probe_acc, probe_weight = carry
        intensity, position = item
        row_at = position[0].astype(jnp.int32)
        col_at = position[1].astype(jnp.int32)
        patch = lax.dynamic_slice(object_field, (anchor, row_at, col_at), (2, W, W))
        exit_wave = probe_cplx * lax.complex(patch[0], patch[1])[None]
        far_field = jnp.fft.fft2(exit_wave, norm="ortho")
        model_int = jnp.sum(far_field.real * far_field.real + far_field.imag * far_field.imag, axis=0)
        weight = 2.0 * (model_int - intensity)
        back_wave = jnp.fft.ifft2(weight[None] * far_field, norm="ortho")
        back_re = back_wave.real
        back_im = back_wave.imag
        numer_re = jnp.sum(probe[:, 0] * back_re + probe[:, 1] * back_im, axis=0)
        numer_im = jnp.sum(probe[:, 0] * back_im - probe[:, 1] * back_re, axis=0)
        grad_image = jnp.stack([numer_re, numer_im, probe_power])
        window = lax.dynamic_slice(object_acc, (anchor, row_at, col_at), (3, W, W))
        object_acc = lax.dynamic_update_slice(object_acc, window + grad_image, (anchor, row_at, col_at))
        patch_re = patch[0][None]
        patch_im = patch[1][None]
        probe_acc = probe_acc + jnp.stack([patch_re * back_re + patch_im * back_im, patch_re * back_im - patch_im * back_re], axis=1)
        probe_weight = probe_weight + patch[0] * patch[0] + patch[1] * patch[1]
        return (object_acc, probe_acc, probe_weight), None

    start = (jnp.zeros((3, ROWS, COLS), jnp.float32), jnp.zeros((MODES, 2, W, W), jnp.float32), jnp.zeros((W, W), jnp.float32))
    (object_acc, probe_acc, probe_weight), _ = lax.scan(visit, start, (measured, positions))
    object_gradient = object_acc[:2] / jnp.maximum(object_acc[2], 1.0)[None]
    probe_gradient = probe_acc / (probe_weight + 1e-5)[None, None]
    return (object_gradient, probe_gradient)
```

```python
import functools
import math

import jax
import jax.numpy as jnp
import numpy as np
from jax import lax
from jax.experimental import pallas as pl
from jax.experimental.pallas import tpu as pltpu
from jax.sharding import PartitionSpec as P

F32 = jnp.float32
BF16 = jnp.bfloat16


def dft_blocks(length):
    steps = np.arange(length)
    angle = (steps[:, None] * steps[None, :] % length) * (2.0 * math.pi / length)
    factor = 1.0 / math.sqrt(length)
    cos = np.cos(angle) * factor
    sin = -np.sin(angle) * factor
    fwd = np.block([[cos, sin], [-sin, cos]]).astype(np.float32)
    inv = np.block([[cos, -sin], [sin, cos]]).astype(np.float32)
    tables = []
    for table in (fwd, inv):
        high = table.astype(jnp.bfloat16)
        low = (table - high.astype(np.float32)).astype(jnp.bfloat16)
        tables += [high, low]
    return np.stack(tables)


def split(x):
    high = x.astype(BF16)
    return high, (x - high.astype(F32)).astype(BF16)


def dot(a, b):
    return jnp.dot(a, b, preferred_element_type=F32)


def wave_kernel(edge, modes, patch, probe, measured, tables, numer, probe_numer, far, model):
    fwd_h, fwd_l, inv_h, inv_l = 0, 1, 2, 3

    def right(x, high_at, low_at):
        high, low = split(x)
        return dot(high, tables[high_at]) + dot(high, tables[low_at]) + dot(low, tables[high_at])

    def left(x, high_at, low_at):
        high, low = split(x)
        return dot(tables[high_at], high) + dot(tables[low_at], high) + dot(tables[high_at], low)

    def rows(x):
        return jnp.concatenate([x[:, :edge], x[:, edge:]], axis=0)

    model[...] = jnp.zeros_like(model)
    numer[...] = jnp.zeros_like(numer)

    def forward(k, carry):
        pr, pi = probe[k, 0], probe[k, 1]
        qr, qi = patch[0], patch[1]
        wave = jnp.concatenate([pr * qr - pi * qi, pr * qi + pi * qr], axis=1)
        out = left(rows(right(wave, fwd_h, fwd_l)), inv_h, inv_l)
        fr, fi = out[:edge], out[edge:]
        far[k, 0] = fr
        far[k, 1] = fi
        model[...] += fr * fr + fi * fi
        return carry

    lax.fori_loop(0, modes, forward, 0)
    model[...] = 2.0 * (model[...] - measured[...])

    def backward(k, carry):
        weight = model[...]
        wave = jnp.concatenate([weight * far[k, 0], weight * far[k, 1]], axis=1)
        out = left(rows(right(wave, inv_h, inv_l)), fwd_h, fwd_l)
        br, bi = out[:edge], out[edge:]
        pr, pi = probe[k, 0], probe[k, 1]
        qr, qi = patch[0], patch[1]
        numer[0] += pr * br + pi * bi
        numer[1] += pr * bi - pi * br
        probe_numer[k, 0] = qr * br + qi * bi
        probe_numer[k, 1] = qr * bi - qi * br
        return carry

    lax.fori_loop(0, modes, backward, 0)


def wave(patch, probe, measured):
    modes, _, edge, _ = probe.shape
    vmem = pl.BlockSpec(memory_space=pltpu.VMEM)
    return pl.pallas_call(
        functools.partial(wave_kernel, edge, modes),
        out_shape=(
            jax.ShapeDtypeStruct((2, edge, edge), F32),
            jax.ShapeDtypeStruct((modes, 2, edge, edge), F32),
        ),
        in_specs=[vmem] * 4,
        out_specs=(vmem, vmem),
        scratch_shapes=[pltpu.VMEM((modes, 2, edge, edge), F32), pltpu.VMEM((edge, edge), F32)],
        compiler_params=pltpu.CompilerParams(vmem_limit_bytes=40 * 2**20),
        cost_estimate=pl.CostEstimate(
            flops=modes * 48 * edge**3 * 2, bytes_accessed=modes * 16 * edge**2, transcendentals=0
        ),
    )(patch, probe, measured, jnp.asarray(dft_blocks(edge)))


def placement(start, offset, size, edge):
    at = start[:, None, None] + lax.broadcasted_iota(jnp.int32, (1, edge, size), 1)
    here = offset + lax.broadcasted_iota(jnp.int32, (1, edge, size), 2)
    return (at == here).astype(BF16)


def split_outside(x):
    high = lax.reduce_precision(x, 8, 7)
    return jnp.stack([high, x - high]).astype(BF16)


def place_exact(images, row_hot, col_hot):
    both = split_outside(images)
    cols = jnp.einsum("hpcab,pbj->hpcaj", both, col_hot, preferred_element_type=F32)
    cols = cols[0] + cols[1]
    both = split_outside(cols)
    out = jnp.einsum("pai,hpcaj->hcij", row_hot, both, preferred_element_type=F32)
    return out[0] + out[1]


def body(object_field, probe, measured, positions):
    strip_rows = object_field.shape[1]
    tile_cols = object_field.shape[2]
    pattern_count = measured.shape[0]
    edge_len = measured.shape[1]
    mode_count = probe.shape[0]
    scan_count = lax.axis_size("scan")
    tile_count = lax.axis_size("tile")
    scan_index = lax.axis_index("scan")
    tile_index = lax.axis_index("tile")
    total_rows = strip_rows * scan_count
    anchor = jnp.zeros((), jnp.int32)
    grid_pos = positions.reshape(scan_count, tile_count, pattern_count, 2)
    column_pos = lax.dynamic_index_in_dim(grid_pos, tile_index, axis=1, keepdims=False)
    row_pos = lax.dynamic_index_in_dim(grid_pos, scan_index, axis=0, keepdims=False)
    row_pos = row_pos.reshape(tile_count, 2)
    own_pos = lax.dynamic_index_in_dim(column_pos, scan_index, axis=0, keepdims=False)
    strip = lax.all_gather(object_field, "tile", axis=2, tiled=True)
    strip_top = scan_index * strip_rows
    tile_left = tile_index * tile_cols

    power = jnp.sum(probe[:, 0] * probe[:, 0] + probe[:, 1] * probe[:, 1], axis=0)
    all_rows = placement(positions[:, 0], strip_top, strip_rows, edge_len)
    all_cols = placement(positions[:, 1], tile_left, tile_cols, edge_len)
    power_all = jnp.broadcast_to(power, (positions.shape[0], 1) + power.shape)
    denom = place_exact(power_all, all_rows, all_cols)[0]
    denom = jnp.maximum(denom, 1.0)

    def cut_slice(position):
        row_at = position[0]
        block_piece = lax.dynamic_slice(
            strip, (anchor, anchor, position[1]), (2, strip_rows, edge_len)
        )
        intersections = jnp.logical_and(
            strip_top < row_at + edge_len, strip_top + strip_rows > row_at
        )
        return jnp.where(intersections, block_piece, 0.0)

    outgoing = jax.vmap(jax.vmap(cut_slice), out_axes=2)(column_pos)
    incoming = lax.all_to_all(outgoing, "scan", split_axis=2, concat_axis=2, tiled=True)
    column = incoming.reshape(2, total_rows, edge_len)
    patch = lax.dynamic_slice(column, (anchor, own_pos[0, 0], anchor), (2, edge_len, edge_len))

    numer, probe_numer = wave(patch, probe, measured[0])
    weight = jnp.sum(patch * patch, axis=0)

    numers = lax.all_gather(numer, "tile", axis=0)
    row_hot = placement(row_pos[:, 0], 0, total_rows, edge_len)
    col_hot = placement(row_pos[:, 1], tile_left, tile_cols, edge_len)
    placed = place_exact(numers, row_hot, col_hot)
    summed = lax.psum_scatter(placed, "scan", scatter_dimension=1, tiled=True)
    object_gradient = summed / denom[None]

    own = lax.psum_scatter(probe_numer, "tile", scatter_dimension=0, tiled=True)
    own = lax.psum(own, "scan")
    weight_all = lax.psum(weight, ("scan", "tile"))
    probe_gradient = own / (weight_all + 1e-05)[None, None]
    return (object_gradient, probe_gradient)


def solution(mesh):
    return jax.shard_map(
        body,
        mesh=mesh,
        in_specs=(
            P(None, ("groups", "scan"), "tile"),
            P("groups", None, None, None),
            P(("groups", "scan", "tile"), None, None),
            P("groups", None),
        ),
        out_specs=(P(None, ("groups", "scan"), "tile"), P(("groups", "tile"), None, None, None)),
        check_vma=False,
    )
```

```python
import functools
import math

import jax
import jax.numpy as jnp
import numpy as np
from jax import lax
from jax.experimental import pallas as pl
from jax.experimental.pallas import tpu as pltpu
from jax.sharding import PartitionSpec as P

F32 = jnp.float32
BF16 = jnp.bfloat16


def dft_blocks(length):
    steps = np.arange(length)
    angle = (steps[:, None] * steps[None, :] % length) * (2.0 * math.pi / length)
    factor = 1.0 / math.sqrt(length)
    cos = np.cos(angle) * factor
    sin = -np.sin(angle) * factor
    fwd = np.block([[cos, sin], [-sin, cos]]).astype(np.float32)
    inv = np.block([[cos, -sin], [sin, cos]]).astype(np.float32)
    tables = []
    for table in (fwd, inv):
        high = table.astype(jnp.bfloat16)
        low = (table - high.astype(np.float32)).astype(jnp.bfloat16)
        tables += [high, low]
    return np.stack(tables)


def split(x):
    high = x.astype(BF16)
    return high, (x - high.astype(F32)).astype(BF16)


def dot(a, b):
    return jnp.dot(a, b, preferred_element_type=F32)


def wave_kernel(edge, modes, patch, probe, measured, tables, numer, probe_numer, far, model):
    fwd_h, fwd_l, inv_h, inv_l = 0, 1, 2, 3

    def right(x, high_at, low_at):
        high, low = split(x)
        return dot(high, tables[high_at]) + dot(high, tables[low_at]) + dot(low, tables[high_at])

    def left(x, high_at, low_at):
        high, low = split(x)
        return dot(tables[high_at], high) + dot(tables[low_at], high) + dot(tables[high_at], low)

    def rows(x):
        return jnp.concatenate([x[:, :edge], x[:, edge:]], axis=0)

    model[...] = jnp.zeros_like(model)
    numer[...] = jnp.zeros_like(numer)

    def forward(k, carry):
        pr, pi = probe[k, 0], probe[k, 1]
        qr, qi = patch[0], patch[1]
        wave = jnp.concatenate([pr * qr - pi * qi, pr * qi + pi * qr], axis=1)
        out = left(rows(right(wave, fwd_h, fwd_l)), inv_h, inv_l)
        fr, fi = out[:edge], out[edge:]
        far[k, 0] = fr
        far[k, 1] = fi
        model[...] += fr * fr + fi * fi
        return carry

    lax.fori_loop(0, modes, forward, 0)
    model[...] = 2.0 * (model[...] - measured[...])

    def backward(k, carry):
        weight = model[...]
        wave = jnp.concatenate([weight * far[k, 0], weight * far[k, 1]], axis=1)
        out = left(rows(right(wave, inv_h, inv_l)), fwd_h, fwd_l)
        br, bi = out[:edge], out[edge:]
        pr, pi = probe[k, 0], probe[k, 1]
        qr, qi = patch[0], patch[1]
        numer[0] += pr * br + pi * bi
        numer[1] += pr * bi - pi * br
        probe_numer[k, 0] = qr * br + qi * bi
        probe_numer[k, 1] = qr * bi - qi * br
        return carry

    lax.fori_loop(0, modes, backward, 0)


def wave(patch, probe, measured):
    modes, _, edge, _ = probe.shape
    vmem = pl.BlockSpec(memory_space=pltpu.VMEM)
    return pl.pallas_call(
        functools.partial(wave_kernel, edge, modes),
        out_shape=(
            jax.ShapeDtypeStruct((2, edge, edge), F32),
            jax.ShapeDtypeStruct((modes, 2, edge, edge), F32),
        ),
        in_specs=[vmem] * 4,
        out_specs=(vmem, vmem),
        scratch_shapes=[pltpu.VMEM((modes, 2, edge, edge), F32), pltpu.VMEM((edge, edge), F32)],
        compiler_params=pltpu.CompilerParams(vmem_limit_bytes=40 * 2**20),
        cost_estimate=pl.CostEstimate(
            flops=modes * 48 * edge**3 * 2, bytes_accessed=modes * 16 * edge**2, transcendentals=0
        ),
    )(patch, probe, measured, jnp.asarray(dft_blocks(edge)))


MESH = pl.DeviceIdType.MESH


def greet(counts):
    barrier = pltpu.get_barrier_semaphore()
    total = 0
    for axis, count in counts:
        me = lax.axis_index(axis)
        for i in range(1, count):
            pl.semaphore_signal(
                barrier, inc=1, device_id={axis: lax.rem(me + i, count)}, device_id_type=MESH
            )
            total += 1
    pl.semaphore_wait(barrier, total)


def push(src, dst, sems, at, axis, peer):
    copy = pltpu.make_async_remote_copy(
        src_ref=src,
        dst_ref=dst,
        send_sem=sems.at[0, at],
        recv_sem=sems.at[1, at],
        device_id={axis: peer},
        device_id_type=MESH,
    )
    copy.start()
    return copy


def first_kernel(
    ns, nt, modes, part_rows, numer, probe_numer, weight, numers, part, weight_part, got, got_w, z_sems, p_sems, w_sems
):
    scan, tile = lax.axis_index("scan"), lax.axis_index("tile")
    greet((("scan", ns), ("tile", nt)))
    copies = []
    for i in range(1, nt):
        peer = lax.rem(tile + i, nt)
        copies.append(push(numer, numers.at[i], z_sems, i - 1, "tile", peer))
    sums = []
    for i in range(1, ns):
        peer = lax.rem(scan + i, ns)
        span = pl.ds(pl.multiple_of(peer * part_rows, part_rows), part_rows)
        sums.append(push(weight.at[span, :], got_w.at[i - 1], w_sems, i - 1, "scan", peer))
        sums.append(push(probe_numer.at[:, :, span, :], got.at[i - 1], p_sems, i - 1, "scan", peer))
    numers[0] = numer[...]
    for copy in sums:
        copy.wait()
    mine = pl.ds(pl.multiple_of(scan * part_rows, part_rows), part_rows)
    total = weight[mine, :]
    for i in range(ns - 1):
        total += got_w[i]
    weight_part[...] = total

    def add(k, carry):
        value = probe_numer[k, :, mine, :]
        for i in range(ns - 1):
            value += got[i, k]
        part[k] = value
        return carry

    lax.fori_loop(0, modes, add, 0)
    for copy in copies:
        copy.wait()


def first(ns, nt, numer, probe_numer, weight):
    modes, _, edge, _ = probe_numer.shape
    part_rows = edge // ns
    vmem = pl.BlockSpec(memory_space=pltpu.VMEM)
    dma = pltpu.SemaphoreType.DMA
    return pl.pallas_call(
        functools.partial(first_kernel, ns, nt, modes, part_rows),
        out_shape=(
            jax.ShapeDtypeStruct((nt, 2, edge, edge), F32),
            jax.ShapeDtypeStruct((modes, 2, part_rows, edge), F32),
            jax.ShapeDtypeStruct((part_rows, edge), F32),
        ),
        in_specs=[vmem] * 3,
        out_specs=(vmem,) * 3,
        scratch_shapes=[
            pltpu.VMEM((ns - 1, modes, 2, part_rows, edge), F32),
            pltpu.VMEM((ns - 1, part_rows, edge), F32),
            dma((2, nt - 1)),
            dma((2, ns - 1)),
            dma((2, ns - 1)),
        ],
        compiler_params=pltpu.CompilerParams(
            collective_id=0, has_side_effects=True, vmem_limit_bytes=40 * 2**20
        ),
    )(numer, probe_numer, weight)


def second_kernel(
    ns, nt, own_modes, part_rows, placed, denom, part, weight_part, grad, probe_grad, got_o, got_p, got_w, o_sems, p_sems, w_sems, g_sems
):
    scan, tile = lax.axis_index("scan"), lax.axis_index("tile")
    greet((("scan", ns), ("tile", nt)))
    probe_copies, object_copies, last = [], [], []
    for i in range(1, nt):
        peer = lax.rem(tile + i, nt)
        span = pl.ds(peer * own_modes, own_modes)
        probe_copies.append(push(weight_part, got_w.at[i - 1], w_sems, i - 1, "tile", peer))
        probe_copies.append(push(part.at[span], got_p.at[i - 1], p_sems, i - 1, "tile", peer))
    for i in range(1, ns):
        peer = lax.rem(scan + i, ns)
        object_copies.append(push(placed.at[peer], got_o.at[i - 1], o_sems, i - 1, "scan", peer))
    for copy in probe_copies:
        copy.wait()
    total = weight_part[...]
    for i in range(nt - 1):
        total += got_w[i]
    scale = 1.0 / (total + 1e-05)
    mine = pl.ds(pl.multiple_of(scan * part_rows, part_rows), part_rows)
    for k in range(own_modes):
        value = part[tile * own_modes + k]
        for i in range(nt - 1):
            value += got_p[i, k]
        probe_grad[k, :, mine, :] = value * scale[None]
    for i in range(1, ns):
        peer = lax.rem(scan + i, ns)
        rows = probe_grad.at[:, :, mine, :]
        last.append(push(rows, rows, g_sems, i - 1, "scan", peer))
    for copy in object_copies:
        copy.wait()
    for c in range(2):
        value = placed[scan, c]
        for i in range(ns - 1):
            value += got_o[i, c]
        grad[c] = value / denom[...]
    for copy in last:
        copy.wait()


def second(ns, nt, placed, denom, part, weight_part):
    modes, _, part_rows, edge = part.shape
    own_modes = modes // nt
    block = placed.shape[1:]
    vmem = pl.BlockSpec(memory_space=pltpu.VMEM)
    dma = pltpu.SemaphoreType.DMA
    return pl.pallas_call(
        functools.partial(second_kernel, ns, nt, own_modes, part_rows),
        out_shape=(
            jax.ShapeDtypeStruct(block, F32),
            jax.ShapeDtypeStruct((own_modes, 2, edge, edge), F32),
        ),
        in_specs=[vmem] * 4,
        out_specs=(vmem,) * 2,
        scratch_shapes=[
            pltpu.VMEM((ns - 1,) + block, F32),
            pltpu.VMEM((nt - 1, own_modes, 2, part_rows, edge), F32),
            pltpu.VMEM((nt - 1, part_rows, edge), F32),
            dma((2, ns - 1)),
            dma((2, nt - 1)),
            dma((2, nt - 1)),
            dma((2, ns - 1)),
        ],
        compiler_params=pltpu.CompilerParams(
            collective_id=1, has_side_effects=True, vmem_limit_bytes=40 * 2**20
        ),
    )(placed, denom, part, weight_part)


def placement(start, offset, size, edge):
    at = start[:, None, None] + lax.broadcasted_iota(jnp.int32, (1, edge, size), 1)
    here = offset + lax.broadcasted_iota(jnp.int32, (1, edge, size), 2)
    return (at == here).astype(BF16)


def split_outside(x):
    high = lax.reduce_precision(x, 8, 7)
    return jnp.stack([high, x - high]).astype(BF16)


def place_exact(images, row_hot, col_hot):
    both = split_outside(images)
    cols = jnp.einsum("hpcab,pbj->hpcaj", both, col_hot, preferred_element_type=F32)
    cols = cols[0] + cols[1]
    both = split_outside(cols)
    out = jnp.einsum("pai,hpcaj->hcij", row_hot, both, preferred_element_type=F32)
    return out[0] + out[1]


def body(object_field, probe, measured, positions):
    strip_rows = object_field.shape[1]
    tile_cols = object_field.shape[2]
    pattern_count = measured.shape[0]
    edge_len = measured.shape[1]
    mode_count = probe.shape[0]
    scan_count = lax.axis_size("scan")
    tile_count = lax.axis_size("tile")
    scan_index = lax.axis_index("scan")
    tile_index = lax.axis_index("tile")
    total_rows = strip_rows * scan_count
    anchor = jnp.zeros((), jnp.int32)
    grid_pos = positions.reshape(scan_count, tile_count, pattern_count, 2)
    column_pos = lax.dynamic_index_in_dim(grid_pos, tile_index, axis=1, keepdims=False)
    row_pos = lax.dynamic_index_in_dim(grid_pos, scan_index, axis=0, keepdims=False)
    row_pos = row_pos.reshape(tile_count, 2)
    own_pos = lax.dynamic_index_in_dim(column_pos, scan_index, axis=0, keepdims=False)
    strip = lax.all_gather(object_field, "tile", axis=2, tiled=True)
    strip_top = scan_index * strip_rows
    tile_left = tile_index * tile_cols

    power = jnp.sum(probe[:, 0] * probe[:, 0] + probe[:, 1] * probe[:, 1], axis=0)
    all_rows = placement(positions[:, 0], strip_top, strip_rows, edge_len)
    all_cols = placement(positions[:, 1], tile_left, tile_cols, edge_len)
    power_all = jnp.broadcast_to(power, (positions.shape[0], 1) + power.shape)
    denom = place_exact(power_all, all_rows, all_cols)[0]
    denom = jnp.maximum(denom, 1.0)

    def cut_slice(position):
        row_at = position[0]
        block_piece = lax.dynamic_slice(
            strip, (anchor, anchor, position[1]), (2, strip_rows, edge_len)
        )
        intersections = jnp.logical_and(
            strip_top < row_at + edge_len, strip_top + strip_rows > row_at
        )
        return jnp.where(intersections, block_piece, 0.0)

    outgoing = jax.vmap(jax.vmap(cut_slice), out_axes=2)(column_pos)
    incoming = lax.all_to_all(outgoing, "scan", split_axis=2, concat_axis=2, tiled=True)
    column = incoming.reshape(2, total_rows, edge_len)
    patch = lax.dynamic_slice(column, (anchor, own_pos[0, 0], anchor), (2, edge_len, edge_len))

    numer, probe_numer = wave(patch, probe, measured[0])
    weight = jnp.sum(patch * patch, axis=0)

    numers, part, weight_part = first(scan_count, tile_count, numer, probe_numer, weight)
    sources = lax.rem(tile_index + tile_count - lax.iota(jnp.int32, tile_count), tile_count)
    row_pos = row_pos[sources]
    row_hot = placement(row_pos[:, 0], 0, total_rows, edge_len)
    col_hot = placement(row_pos[:, 1], tile_left, tile_cols, edge_len)
    placed = place_exact(numers, row_hot, col_hot)
    placed = placed.reshape(2, scan_count, strip_rows, tile_cols).transpose(1, 0, 2, 3)
    object_gradient, probe_gradient = second(
        scan_count, tile_count, placed, denom, part, weight_part
    )
    return (object_gradient, probe_gradient)


def solution(mesh):
    return jax.shard_map(
        body,
        mesh=mesh,
        in_specs=(
            P(None, ("groups", "scan"), "tile"),
            P("groups", None, None, None),
            P(("groups", "scan", "tile"), None, None),
            P("groups", None),
        ),
        out_specs=(P(None, ("groups", "scan"), "tile"), P(("groups", "tile"), None, None, None)),
        check_vma=False,
    )
```

```python
import functools
import math

import jax
import jax.numpy as jnp
import numpy as np
from jax import lax
from jax.experimental import pallas as pl
from jax.experimental.pallas import tpu as pltpu
from jax.sharding import PartitionSpec as P

F32 = jnp.float32
BF16 = jnp.bfloat16


def dft_blocks(length):
    steps = np.arange(length)
    angle = (steps[:, None] * steps[None, :] % length) * (2.0 * math.pi / length)
    factor = 1.0 / math.sqrt(length)
    cos = np.cos(angle) * factor
    sin = -np.sin(angle) * factor
    fwd = np.block([[cos, sin], [-sin, cos]]).astype(np.float32)
    inv = np.block([[cos, -sin], [sin, cos]]).astype(np.float32)
    tables = []
    for table in (fwd, inv):
        high = table.astype(jnp.bfloat16)
        low = (table - high.astype(np.float32)).astype(jnp.bfloat16)
        tables += [high, low]
    return np.stack(tables)


def split(x):
    high = x.astype(BF16)
    return high, (x - high.astype(F32)).astype(BF16)


def dot(a, b):
    return jnp.dot(a, b, preferred_element_type=F32)


def wave_kernel(edge, modes, patch, probe, measured, tables, numer, probe_numer, far, model):
    fwd_h, fwd_l, inv_h, inv_l = 0, 1, 2, 3

    def right(x, high_at, low_at):
        high, low = split(x)
        return dot(high, tables[high_at]) + dot(high, tables[low_at]) + dot(low, tables[high_at])

    def left(x, high_at, low_at):
        high, low = split(x)
        return dot(tables[high_at], high) + dot(tables[low_at], high) + dot(tables[high_at], low)

    def rows(x):
        return jnp.concatenate([x[:, :edge], x[:, edge:]], axis=0)

    model[...] = jnp.zeros_like(model)
    numer[...] = jnp.zeros_like(numer)

    def forward(k, carry):
        pr, pi = probe[k, 0], probe[k, 1]
        qr, qi = patch[0], patch[1]
        wave = jnp.concatenate([pr * qr - pi * qi, pr * qi + pi * qr], axis=1)
        out = left(rows(right(wave, fwd_h, fwd_l)), inv_h, inv_l)
        fr, fi = out[:edge], out[edge:]
        far[k, 0] = fr
        far[k, 1] = fi
        model[...] += fr * fr + fi * fi
        return carry

    lax.fori_loop(0, modes, forward, 0)
    model[...] = 2.0 * (model[...] - measured[...])

    def backward(k, carry):
        weight = model[...]
        wave = jnp.concatenate([weight * far[k, 0], weight * far[k, 1]], axis=1)
        out = left(rows(right(wave, inv_h, inv_l)), fwd_h, fwd_l)
        br, bi = out[:edge], out[edge:]
        pr, pi = probe[k, 0], probe[k, 1]
        qr, qi = patch[0], patch[1]
        numer[0] += pr * br + pi * bi
        numer[1] += pr * bi - pi * br
        probe_numer[k, 0] = qr * br + qi * bi
        probe_numer[k, 1] = qr * bi - qi * br
        return carry

    lax.fori_loop(0, modes, backward, 0)


def wave(patch, probe, measured):
    modes, _, edge, _ = probe.shape
    vmem = pl.BlockSpec(memory_space=pltpu.VMEM)
    return pl.pallas_call(
        functools.partial(wave_kernel, edge, modes),
        out_shape=(
            jax.ShapeDtypeStruct((2, edge, edge), F32),
            jax.ShapeDtypeStruct((modes, 2, edge, edge), F32),
        ),
        in_specs=[vmem] * 4,
        out_specs=(vmem, vmem),
        scratch_shapes=[pltpu.VMEM((modes, 2, edge, edge), F32), pltpu.VMEM((edge, edge), F32)],
        compiler_params=pltpu.CompilerParams(vmem_limit_bytes=40 * 2**20),
        cost_estimate=pl.CostEstimate(
            flops=modes * 48 * edge**3 * 2, bytes_accessed=modes * 16 * edge**2, transcendentals=0
        ),
    )(patch, probe, measured, jnp.asarray(dft_blocks(edge)))


MESH = pl.DeviceIdType.MESH


def greet(counts):
    barrier = pltpu.get_barrier_semaphore()
    total = 0
    for axis, count in counts:
        me = lax.axis_index(axis)
        for i in range(1, count):
            pl.semaphore_signal(
                barrier, inc=1, device_id={axis: lax.rem(me + i, count)}, device_id_type=MESH
            )
            total += 1
    pl.semaphore_wait(barrier, total)


def push(src, dst, sems, at, axis, peer):
    copy = pltpu.make_async_remote_copy(
        src_ref=src,
        dst_ref=dst,
        send_sem=sems.at[0, at],
        recv_sem=sems.at[1, at],
        device_id={axis: peer},
        device_id_type=MESH,
    )
    copy.start()
    return copy


def relay(nt, slots, sems):
    tile = lax.axis_index("tile")

    def copy(slot, way, hop, peer):
        at = jnp.clip(slot, 0, nt - 1)
        return pltpu.make_async_remote_copy(
            src_ref=slots.at[at],
            dst_ref=slots.at[at],
            send_sem=sems.at[0, way, hop],
            recv_sem=sems.at[1, way, hop],
            device_id={"tile": jnp.clip(peer, 0, nt - 1)},
            device_id_type=MESH,
        )

    def sends(hop, act):
        pl.when(jnp.logical_and(tile + 1 < nt, tile - hop >= 0))(
            lambda: act(copy(tile - hop, 0, hop, tile + 1))
        )
        pl.when(jnp.logical_and(tile - 1 >= 0, tile + hop < nt))(
            lambda: act(copy(tile + hop, 1, hop, tile - 1))
        )

    def start(hop):
        sends(hop, lambda c: c.start())

    def finish(hop):
        sends(hop, lambda c: c.wait_send())

    def receive(hop):
        pl.when(tile - 1 - hop >= 0)(lambda: copy(tile - 1 - hop, 0, hop, tile - 1).wait_recv())
        pl.when(tile + 1 + hop < nt)(lambda: copy(tile + 1 + hop, 1, hop, tile + 1).wait_recv())

    return start, receive, finish


def hot(shape, row_start, col_start):
    rows = row_start + lax.broadcasted_iota(jnp.int32, shape, 0)
    cols = col_start + lax.broadcasted_iota(jnp.int32, shape, 1)
    return (rows == cols).astype(F32).astype(BF16)


def cut_kernel(
    ns, nt, positions, tile_ref, probe, patch, denom, tiles, pieces, got, power, t_sems, s_sems
):
    scan, tile = lax.axis_index("scan"), lax.axis_index("tile")
    strip_rows, tile_cols = tile_ref.shape[1:]
    edge = patch.shape[1]
    modes = probe.shape[0]
    greet((("scan", ns), ("tile", nt)))
    tiles[tile] = tile_ref[...]
    start, receive, finish = relay(nt, tiles, t_sems)
    start(0)
    pieces[...] = jnp.zeros_like(pieces)

    def cut(slot):
        high, low = split(tiles[slot].reshape(2 * strip_rows, tile_cols))

        def one(i, carry):
            col_at = positions[i * nt + tile, 1]
            pick = hot((tile_cols, edge), slot * tile_cols, col_at)
            pieces[i] += (dot(high, pick) + dot(low, pick)).reshape(2, strip_rows, edge)
            return carry

        lax.fori_loop(0, ns, one, 0)

    cut(tile)
    power[...] = jnp.zeros_like(power)

    def add_power(k, carry):
        power[...] += probe[k, 0] * probe[k, 0] + probe[k, 1] * probe[k, 1]
        return carry

    lax.fori_loop(0, modes, add_power, 0)
    denom[...] = jnp.zeros_like(denom)

    def add_weight(j, carry):
        row_pick = hot((strip_rows, edge), scan * strip_rows, positions[j, 0])
        col_pick = hot((edge, tile_cols), positions[j, 1], tile * tile_cols)
        high, low = split(power[...])
        rows = dot(row_pick, high) + dot(row_pick, low)
        high, low = split(rows)
        denom[...] += dot(high, col_pick) + dot(low, col_pick)
        return carry

    lax.fori_loop(0, positions.shape[0], add_weight, 0)
    denom[...] = jnp.maximum(denom[...], 1.0)
    for hop in range(nt - 1):
        receive(hop)
        if hop + 1 < nt - 1:
            start(hop + 1)
        pl.when(tile - 1 - hop >= 0)(lambda: cut(jnp.maximum(tile - 1 - hop, 0)))
        pl.when(tile + 1 + hop < nt)(lambda: cut(jnp.minimum(tile + 1 + hop, nt - 1)))
    copies = []
    for i in range(1, ns):
        peer = lax.rem(scan + i, ns)
        copies.append(push(pieces.at[peer], got.at[i - 1], s_sems, i - 1, "scan", peer))
    row_at = positions[scan * nt + tile, 0]

    def add_rows(piece, source):
        pick = hot((edge, strip_rows), row_at, source * strip_rows)
        out = []
        for c in range(2):
            high, low = split(piece[c])
            out.append(dot(pick, high) + dot(pick, low))
        return jnp.stack(out)

    patch[...] = add_rows(pieces[scan], scan)
    for copy in copies:
        copy.wait()
    for i in range(1, ns):
        patch[...] += add_rows(got[i - 1], lax.rem(scan + ns - i, ns))
    for hop in range(nt - 1):
        finish(hop)


def cut(ns, nt, positions, tile_block, probe):
    _, strip_rows, tile_cols = tile_block.shape
    edge = probe.shape[2]
    vmem = pl.BlockSpec(memory_space=pltpu.VMEM)
    dma = pltpu.SemaphoreType.DMA
    return pl.pallas_call(
        functools.partial(cut_kernel, ns, nt),
        out_shape=(
            jax.ShapeDtypeStruct((2, edge, edge), F32),
            jax.ShapeDtypeStruct((strip_rows, tile_cols), F32),
        ),
        in_specs=[pl.BlockSpec(memory_space=pltpu.SMEM), vmem, vmem],
        out_specs=(vmem,) * 2,
        scratch_shapes=[
            pltpu.VMEM((nt, 2, strip_rows, tile_cols), F32),
            pltpu.VMEM((ns, 2, strip_rows, edge), F32),
            pltpu.VMEM((ns - 1, 2, strip_rows, edge), F32),
            pltpu.VMEM((edge, edge), F32),
            dma((2, 2, nt - 1)),
            dma((2, ns - 1)),
        ],
        compiler_params=pltpu.CompilerParams(
            collective_id=2, has_side_effects=True, vmem_limit_bytes=40 * 2**20
        ),
    )(positions, tile_block, probe)


def first_kernel(
    ns, nt, modes, part_rows, numer, probe_numer, weight, numers, part, weight_part, got, got_w, z_sems, p_sems, w_sems
):
    scan, tile = lax.axis_index("scan"), lax.axis_index("tile")
    greet((("scan", ns), ("tile", nt)))
    numers[tile] = numer[...]
    start, receive, finish = relay(nt, numers, z_sems)
    start(0)
    sums = []
    for i in range(1, ns):
        peer = lax.rem(scan + i, ns)
        span = pl.ds(pl.multiple_of(peer * part_rows, part_rows), part_rows)
        sums.append(push(weight.at[span, :], got_w.at[i - 1], w_sems, i - 1, "scan", peer))
        sums.append(push(probe_numer.at[:, :, span, :], got.at[i - 1], p_sems, i - 1, "scan", peer))
    for hop in range(nt - 1):
        receive(hop)
        if hop + 1 < nt - 1:
            start(hop + 1)
    for copy in sums:
        copy.wait()
    mine = pl.ds(pl.multiple_of(scan * part_rows, part_rows), part_rows)
    total = weight[mine, :]
    for i in range(ns - 1):
        total += got_w[i]
    weight_part[...] = total

    def add(k, carry):
        value = probe_numer[k, :, mine, :]
        for i in range(ns - 1):
            value += got[i, k]
        part[k] = value
        return carry

    lax.fori_loop(0, modes, add, 0)
    for hop in range(nt - 1):
        finish(hop)


def first(ns, nt, numer, probe_numer, weight):
    modes, _, edge, _ = probe_numer.shape
    part_rows = edge // ns
    vmem = pl.BlockSpec(memory_space=pltpu.VMEM)
    dma = pltpu.SemaphoreType.DMA
    return pl.pallas_call(
        functools.partial(first_kernel, ns, nt, modes, part_rows),
        out_shape=(
            jax.ShapeDtypeStruct((nt, 2, edge, edge), F32),
            jax.ShapeDtypeStruct((modes, 2, part_rows, edge), F32),
            jax.ShapeDtypeStruct((part_rows, edge), F32),
        ),
        in_specs=[vmem] * 3,
        out_specs=(vmem,) * 3,
        scratch_shapes=[
            pltpu.VMEM((ns - 1, modes, 2, part_rows, edge), F32),
            pltpu.VMEM((ns - 1, part_rows, edge), F32),
            dma((2, 2, nt - 1)),
            dma((2, ns - 1)),
            dma((2, ns - 1)),
        ],
        compiler_params=pltpu.CompilerParams(
            collective_id=0, has_side_effects=True, vmem_limit_bytes=40 * 2**20
        ),
    )(numer, probe_numer, weight)


def second_kernel(
    ns, nt, own_modes, part_rows, placed, denom, part, weight_part, grad, probe_grad, got_o, got_p, got_w, o_sems, p_sems, w_sems, g_sems
):
    scan, tile = lax.axis_index("scan"), lax.axis_index("tile")
    greet((("scan", ns), ("tile", nt)))
    probe_copies, object_copies, last = [], [], []
    for i in range(1, nt):
        peer = lax.rem(tile + i, nt)
        span = pl.ds(peer * own_modes, own_modes)
        probe_copies.append(push(weight_part, got_w.at[i - 1], w_sems, i - 1, "tile", peer))
        probe_copies.append(push(part.at[span], got_p.at[i - 1], p_sems, i - 1, "tile", peer))
    for i in range(1, ns):
        peer = lax.rem(scan + i, ns)
        object_copies.append(push(placed.at[peer], got_o.at[i - 1], o_sems, i - 1, "scan", peer))
    for copy in probe_copies:
        copy.wait()
    total = weight_part[...]
    for i in range(nt - 1):
        total += got_w[i]
    scale = 1.0 / (total + 1e-05)
    mine = pl.ds(pl.multiple_of(scan * part_rows, part_rows), part_rows)
    for k in range(own_modes):
        value = part[tile * own_modes + k]
        for i in range(nt - 1):
            value += got_p[i, k]
        probe_grad[k, :, mine, :] = value * scale[None]
    for i in range(1, ns):
        peer = lax.rem(scan + i, ns)
        rows = probe_grad.at[:, :, mine, :]
        last.append(push(rows, rows, g_sems, i - 1, "scan", peer))
    for copy in object_copies:
        copy.wait()
    for c in range(2):
        value = placed[scan, c]
        for i in range(ns - 1):
            value += got_o[i, c]
        grad[c] = value / denom[...]
    for copy in last:
        copy.wait()


def second(ns, nt, placed, denom, part, weight_part):
    modes, _, part_rows, edge = part.shape
    own_modes = modes // nt
    block = placed.shape[1:]
    vmem = pl.BlockSpec(memory_space=pltpu.VMEM)
    dma = pltpu.SemaphoreType.DMA
    return pl.pallas_call(
        functools.partial(second_kernel, ns, nt, own_modes, part_rows),
        out_shape=(
            jax.ShapeDtypeStruct(block, F32),
            jax.ShapeDtypeStruct((own_modes, 2, edge, edge), F32),
        ),
        in_specs=[vmem] * 4,
        out_specs=(vmem,) * 2,
        scratch_shapes=[
            pltpu.VMEM((ns - 1,) + block, F32),
            pltpu.VMEM((nt - 1, own_modes, 2, part_rows, edge), F32),
            pltpu.VMEM((nt - 1, part_rows, edge), F32),
            dma((2, ns - 1)),
            dma((2, nt - 1)),
            dma((2, nt - 1)),
            dma((2, ns - 1)),
        ],
        compiler_params=pltpu.CompilerParams(
            collective_id=1, has_side_effects=True, vmem_limit_bytes=40 * 2**20
        ),
    )(placed, denom, part, weight_part)


def placement(start, offset, size, edge):
    at = start[:, None, None] + lax.broadcasted_iota(jnp.int32, (1, edge, size), 1)
    here = offset + lax.broadcasted_iota(jnp.int32, (1, edge, size), 2)
    return (at == here).astype(BF16)


def split_outside(x):
    high = lax.reduce_precision(x, 8, 7)
    return jnp.stack([high, x - high]).astype(BF16)


def place_exact(images, row_hot, col_hot):
    both = split_outside(images)
    cols = jnp.einsum("hpcab,pbj->hpcaj", both, col_hot, preferred_element_type=F32)
    cols = cols[0] + cols[1]
    both = split_outside(cols)
    out = jnp.einsum("pai,hpcaj->hcij", row_hot, both, preferred_element_type=F32)
    return out[0] + out[1]


def body(object_field, probe, measured, positions):
    strip_rows = object_field.shape[1]
    tile_cols = object_field.shape[2]
    pattern_count = measured.shape[0]
    edge_len = measured.shape[1]
    scan_count = lax.axis_size("scan")
    tile_count = lax.axis_size("tile")
    scan_index = lax.axis_index("scan")
    tile_index = lax.axis_index("tile")
    total_rows = strip_rows * scan_count
    grid_pos = positions.reshape(scan_count, tile_count, pattern_count, 2)
    row_pos = lax.dynamic_index_in_dim(grid_pos, scan_index, axis=0, keepdims=False)
    row_pos = row_pos.reshape(tile_count, 2)
    tile_left = tile_index * tile_cols
    patch, denom = cut(scan_count, tile_count, positions, object_field, probe)

    numer, probe_numer = wave(patch, probe, measured[0])
    weight = jnp.sum(patch * patch, axis=0)

    numers, part, weight_part = first(scan_count, tile_count, numer, probe_numer, weight)
    row_hot = placement(row_pos[:, 0], 0, total_rows, edge_len)
    col_hot = placement(row_pos[:, 1], tile_left, tile_cols, edge_len)
    placed = place_exact(numers, row_hot, col_hot)
    placed = placed.reshape(2, scan_count, strip_rows, tile_cols).transpose(1, 0, 2, 3)
    object_gradient, probe_gradient = second(
        scan_count, tile_count, placed, denom, part, weight_part
    )
    return (object_gradient, probe_gradient)


def solution(mesh):
    return jax.shard_map(
        body,
        mesh=mesh,
        in_specs=(
            P(None, ("groups", "scan"), "tile"),
            P("groups", None, None, None),
            P(("groups", "scan", "tile"), None, None),
            P("groups", None),
        ),
        out_specs=(P(None, ("groups", "scan"), "tile"), P(("groups", "tile"), None, None, None)),
        check_vma=False,
    )
```

```python
import functools
import math

import jax
import jax.numpy as jnp
import numpy as np
from jax import lax
from jax.experimental import pallas as pl
from jax.experimental.pallas import tpu as pltpu
from jax.sharding import PartitionSpec as P

F32 = jnp.float32
BF16 = jnp.bfloat16


def dft_blocks(length):
    steps = np.arange(length)
    angle = (steps[:, None] * steps[None, :] % length) * (2.0 * math.pi / length)
    factor = 1.0 / math.sqrt(length)
    cos = np.cos(angle) * factor
    sin = -np.sin(angle) * factor
    fwd = np.block([[cos, sin], [-sin, cos]]).astype(np.float32)
    inv = np.block([[cos, -sin], [sin, cos]]).astype(np.float32)
    tables = []
    for table in (fwd, inv):
        high = table.astype(jnp.bfloat16)
        low = (table - high.astype(np.float32)).astype(jnp.bfloat16)
        tables += [high, low]
    return np.stack(tables)


def split(x):
    high = x.astype(BF16)
    return high, (x - high.astype(F32)).astype(BF16)


def dot(a, b):
    return jnp.dot(a, b, preferred_element_type=F32)


def wave_steps(edge, modes, patch, probe, measured, tables, numer, probe_numer, far, model, done):
    fwd_h, fwd_l, inv_h, inv_l = 0, 1, 2, 3

    def right(x, high_at, low_at):
        high, low = split(x)
        return dot(high, tables[high_at]) + dot(high, tables[low_at]) + dot(low, tables[high_at])

    def left(x, high_at, low_at):
        high, low = split(x)
        return dot(tables[high_at], high) + dot(tables[low_at], high) + dot(tables[high_at], low)

    def rows(x):
        return jnp.concatenate([x[:, :edge], x[:, edge:]], axis=0)

    model[...] = jnp.zeros_like(model)
    numer[...] = jnp.zeros_like(numer)

    def forward(k, carry):
        pr, pi = probe[k, 0], probe[k, 1]
        qr, qi = patch[0], patch[1]
        wave = jnp.concatenate([pr * qr - pi * qi, pr * qi + pi * qr], axis=1)
        out = left(rows(right(wave, fwd_h, fwd_l)), inv_h, inv_l)
        fr, fi = out[:edge], out[edge:]
        far[k, 0] = fr
        far[k, 1] = fi
        model[...] += fr * fr + fi * fi
        return carry

    lax.fori_loop(0, modes, forward, 0)
    model[...] = 2.0 * (model[...] - measured[...])

    def backward(k, carry):
        weight = model[...]
        wave = jnp.concatenate([weight * far[k, 0], weight * far[k, 1]], axis=1)
        out = left(rows(right(wave, inv_h, inv_l)), fwd_h, fwd_l)
        br, bi = out[:edge], out[edge:]
        pr, pi = probe[k, 0], probe[k, 1]
        qr, qi = patch[0], patch[1]
        numer[0] += pr * br + pi * bi
        numer[1] += pr * bi - pi * br
        probe_numer[k, 0] = qr * br + qi * bi
        probe_numer[k, 1] = qr * bi - qi * br
        done(k)
        return carry

    lax.fori_loop(0, modes, backward, 0)


MESH = pl.DeviceIdType.MESH


def greet(counts):
    barrier = pltpu.get_barrier_semaphore()
    total = 0
    for axis, count in counts:
        me = lax.axis_index(axis)
        for i in range(1, count):
            pl.semaphore_signal(
                barrier, inc=1, device_id={axis: lax.rem(me + i, count)}, device_id_type=MESH
            )
            total += 1
    pl.semaphore_wait(barrier, total)


def push(src, dst, sems, at, axis, peer):
    copy = pltpu.make_async_remote_copy(
        src_ref=src,
        dst_ref=dst,
        send_sem=sems.at[0, at],
        recv_sem=sems.at[1, at],
        device_id={axis: peer},
        device_id_type=MESH,
    )
    copy.start()
    return copy


def relay(nt, slots, sems):
    tile = lax.axis_index("tile")

    def copy(slot, way, hop, peer):
        at = jnp.clip(slot, 0, nt - 1)
        return pltpu.make_async_remote_copy(
            src_ref=slots.at[at],
            dst_ref=slots.at[at],
            send_sem=sems.at[0, way, hop],
            recv_sem=sems.at[1, way, hop],
            device_id={"tile": jnp.clip(peer, 0, nt - 1)},
            device_id_type=MESH,
        )

    def sends(hop, act):
        pl.when(jnp.logical_and(tile + 1 < nt, tile - hop >= 0))(
            lambda: act(copy(tile - hop, 0, hop, tile + 1))
        )
        pl.when(jnp.logical_and(tile - 1 >= 0, tile + hop < nt))(
            lambda: act(copy(tile + hop, 1, hop, tile - 1))
        )

    def start(hop):
        sends(hop, lambda c: c.start())

    def finish(hop):
        sends(hop, lambda c: c.wait_send())

    def receive(hop):
        pl.when(tile - 1 - hop >= 0)(lambda: copy(tile - 1 - hop, 0, hop, tile - 1).wait_recv())
        pl.when(tile + 1 + hop < nt)(lambda: copy(tile + 1 + hop, 1, hop, tile + 1).wait_recv())

    return start, receive, finish


def hot(shape, row_start, col_start):
    rows = row_start + lax.broadcasted_iota(jnp.int32, shape, 0)
    cols = col_start + lax.broadcasted_iota(jnp.int32, shape, 1)
    return (rows == cols).astype(F32).astype(BF16)


def cut_kernel(
    ns, nt, positions, tile_ref, probe, patch, denom, tiles, pieces, got, power, t_sems, s_sems
):
    scan, tile = lax.axis_index("scan"), lax.axis_index("tile")
    strip_rows, tile_cols = tile_ref.shape[1:]
    edge = patch.shape[1]
    modes = probe.shape[0]
    greet((("scan", ns), ("tile", nt)))
    tiles[tile] = tile_ref[...]
    start, receive, finish = relay(nt, tiles, t_sems)
    start(0)
    pieces[...] = jnp.zeros_like(pieces)

    def cut(slot):
        high, low = split(tiles[slot].reshape(2 * strip_rows, tile_cols))

        def one(i, carry):
            col_at = positions[i * nt + tile, 1]
            pick = hot((tile_cols, edge), slot * tile_cols, col_at)
            pieces[i] += (dot(high, pick) + dot(low, pick)).reshape(2, strip_rows, edge)
            return carry

        lax.fori_loop(0, ns, one, 0)

    cut(tile)
    power[...] = jnp.zeros_like(power)

    def add_power(k, carry):
        power[...] += probe[k, 0] * probe[k, 0] + probe[k, 1] * probe[k, 1]
        return carry

    lax.fori_loop(0, modes, add_power, 0)
    denom[...] = jnp.zeros_like(denom)

    def add_weight(j, carry):
        row_pick = hot((strip_rows, edge), scan * strip_rows, positions[j, 0])
        col_pick = hot((edge, tile_cols), positions[j, 1], tile * tile_cols)
        high, low = split(power[...])
        rows = dot(row_pick, high) + dot(row_pick, low)
        high, low = split(rows)
        denom[...] += dot(high, col_pick) + dot(low, col_pick)
        return carry

    lax.fori_loop(0, positions.shape[0], add_weight, 0)
    denom[...] = jnp.maximum(denom[...], 1.0)
    for hop in range(nt - 1):
        receive(hop)
        if hop + 1 < nt - 1:
            start(hop + 1)
        pl.when(tile - 1 - hop >= 0)(lambda: cut(jnp.maximum(tile - 1 - hop, 0)))
        pl.when(tile + 1 + hop < nt)(lambda: cut(jnp.minimum(tile + 1 + hop, nt - 1)))
    copies = []
    for i in range(1, ns):
        peer = lax.rem(scan + i, ns)
        copies.append(push(pieces.at[peer], got.at[i - 1], s_sems, i - 1, "scan", peer))
    row_at = positions[scan * nt + tile, 0]

    def add_rows(piece, source):
        pick = hot((edge, strip_rows), row_at, source * strip_rows)
        out = []
        for c in range(2):
            high, low = split(piece[c])
            out.append(dot(pick, high) + dot(pick, low))
        return jnp.stack(out)

    patch[...] = add_rows(pieces[scan], scan)
    for copy in copies:
        copy.wait()
    for i in range(1, ns):
        patch[...] += add_rows(got[i - 1], lax.rem(scan + ns - i, ns))
    for hop in range(nt - 1):
        finish(hop)


def cut(ns, nt, positions, tile_block, probe):
    _, strip_rows, tile_cols = tile_block.shape
    edge = probe.shape[2]
    vmem = pl.BlockSpec(memory_space=pltpu.VMEM)
    dma = pltpu.SemaphoreType.DMA
    return pl.pallas_call(
        functools.partial(cut_kernel, ns, nt),
        out_shape=(
            jax.ShapeDtypeStruct((2, edge, edge), F32),
            jax.ShapeDtypeStruct((strip_rows, tile_cols), F32),
        ),
        in_specs=[pl.BlockSpec(memory_space=pltpu.SMEM), vmem, vmem],
        out_specs=(vmem,) * 2,
        scratch_shapes=[
            pltpu.VMEM((nt, 2, strip_rows, tile_cols), F32),
            pltpu.VMEM((ns, 2, strip_rows, edge), F32),
            pltpu.VMEM((ns - 1, 2, strip_rows, edge), F32),
            pltpu.VMEM((edge, edge), F32),
            dma((2, 2, nt - 1)),
            dma((2, ns - 1)),
        ],
        compiler_params=pltpu.CompilerParams(
            collective_id=2, has_side_effects=True, vmem_limit_bytes=40 * 2**20
        ),
    )(positions, tile_block, probe)


def row_block(ns, scan, part_rows):
    at = lax.rem(scan, 2) * (ns // 2) + scan // 2
    return pl.ds(pl.multiple_of(at * part_rows, part_rows), part_rows)


def first_kernel(
    ns, nt, modes, part_rows, patch, probe, measured, tables, numers, part, weight_part,
    far, model, numer, probe_numer, weight, got_c, half, got_x, got_w,
    z_sems, c_sems, x_sems, w_sems,
):
    scan, tile = lax.axis_index("scan"), lax.axis_index("tile")
    core, column, nx = lax.rem(scan, 2), scan // 2, ns // 2
    edge = patch.shape[1]
    half_rows = nx * part_rows
    greet((("scan", ns), ("tile", nt)))
    weight[...] = patch[0] * patch[0] + patch[1] * patch[1]
    weights = []
    for i in range(1, ns):
        peer = lax.rem(scan + i, ns)
        rows = weight.at[row_block(ns, peer, part_rows), :]
        weights.append(push(rows, got_w.at[i - 1], w_sems, i - 1, "scan", peer))

    def to_core(k):
        rows = pl.ds(pl.multiple_of((1 - core) * half_rows, half_rows), half_rows)
        return pltpu.make_async_remote_copy(
            src_ref=probe_numer.at[k, :, rows, :],
            dst_ref=got_c.at[k],
            send_sem=c_sems.at[0, k],
            recv_sem=c_sems.at[1, k],
            device_id={"scan": scan + 1 - 2 * core},
            device_id_type=MESH,
        )

    def to_chip(k, i):
        peer = lax.rem(column + i, nx)
        rows = pl.ds(pl.multiple_of(peer * part_rows, part_rows), part_rows)
        return pltpu.make_async_remote_copy(
            src_ref=half.at[k, :, rows, :],
            dst_ref=got_x.at[i - 1, k],
            send_sem=x_sems.at[0, i - 1, k],
            recv_sem=x_sems.at[1, i - 1, k],
            device_id={"scan": peer * 2 + core},
            device_id_type=MESH,
        )

    def pass_on(k):
        to_core(k).wait()
        rows = pl.ds(pl.multiple_of(core * half_rows, half_rows), half_rows)
        half[k] = probe_numer[k, :, rows, :] + got_c[k]
        for i in range(1, nx):
            to_chip(k, i).start()

    def done(k):
        to_core(k).start()
        pl.when(k >= 2)(lambda: pass_on(jnp.maximum(k - 2, 0)))

    wave_steps(edge, modes, patch, probe, measured, tables, numer, probe_numer, far, model, done)
    numers[tile] = numer[...]
    start, receive, finish = relay(nt, numers, z_sems)
    start(0)
    for k in range(max(modes - 2, 0), modes):
        pass_on(k)
    for hop in range(nt - 1):
        receive(hop)
        if hop + 1 < nt - 1:
            start(hop + 1)
    for copy in weights:
        copy.wait()
    total = weight[row_block(ns, scan, part_rows), :]
    for i in range(ns - 1):
        total += got_w[i]
    weight_part[...] = total

    def add(k, carry):
        rows = pl.ds(pl.multiple_of(column * part_rows, part_rows), part_rows)
        for i in range(1, nx):
            to_chip(k, i).wait()
        value = half[k, :, rows, :]
        for i in range(nx - 1):
            value += got_x[i, k]
        part[k] = value
        return carry

    lax.fori_loop(0, modes, add, 0)
    for hop in range(nt - 1):
        finish(hop)


def first(ns, nt, patch, probe, measured):
    modes, _, edge, _ = probe.shape
    part_rows = edge // ns
    nx = ns // 2
    half_rows = nx * part_rows
    vmem = pl.BlockSpec(memory_space=pltpu.VMEM)
    dma = pltpu.SemaphoreType.DMA
    return pl.pallas_call(
        functools.partial(first_kernel, ns, nt, modes, part_rows),
        out_shape=(
            jax.ShapeDtypeStruct((nt, 2, edge, edge), F32),
            jax.ShapeDtypeStruct((modes, 2, part_rows, edge), F32),
            jax.ShapeDtypeStruct((part_rows, edge), F32),
        ),
        in_specs=[vmem] * 4,
        out_specs=(vmem,) * 3,
        scratch_shapes=[
            pltpu.VMEM((modes, 2, edge, edge), F32),
            pltpu.VMEM((edge, edge), F32),
            pltpu.VMEM((2, edge, edge), F32),
            pltpu.VMEM((modes, 2, edge, edge), F32),
            pltpu.VMEM((edge, edge), F32),
            pltpu.VMEM((modes, 2, half_rows, edge), F32),
            pltpu.VMEM((modes, 2, half_rows, edge), F32),
            pltpu.VMEM((nx - 1, modes, 2, part_rows, edge), F32),
            pltpu.VMEM((ns - 1, part_rows, edge), F32),
            dma((2, 2, nt - 1)),
            dma((2, modes)),
            dma((2, nx - 1, modes)),
            dma((2, ns - 1)),
        ],
        compiler_params=pltpu.CompilerParams(
            collective_id=0, has_side_effects=True, vmem_limit_bytes=48 * 2**20
        ),
    )(patch, probe, measured, jnp.asarray(dft_blocks(edge)))


def second_kernel(
    ns, nt, own_modes, part_rows, placed, denom, part, weight_part, grad, probe_grad, got_o, got_p, got_w, o_sems, p_sems, w_sems, g_sems
):
    scan, tile = lax.axis_index("scan"), lax.axis_index("tile")
    greet((("scan", ns), ("tile", nt)))
    probe_copies, object_copies, last = [], [], []
    for i in range(1, nt):
        peer = lax.rem(tile + i, nt)
        span = pl.ds(peer * own_modes, own_modes)
        probe_copies.append(push(weight_part, got_w.at[i - 1], w_sems, i - 1, "tile", peer))
        probe_copies.append(push(part.at[span], got_p.at[i - 1], p_sems, i - 1, "tile", peer))
    for i in range(1, ns):
        peer = lax.rem(scan + i, ns)
        object_copies.append(push(placed.at[peer], got_o.at[i - 1], o_sems, i - 1, "scan", peer))
    for copy in probe_copies:
        copy.wait()
    total = weight_part[...]
    for i in range(nt - 1):
        total += got_w[i]
    scale = 1.0 / (total + 1e-05)
    mine = row_block(ns, scan, part_rows)
    for k in range(own_modes):
        value = part[tile * own_modes + k]
        for i in range(nt - 1):
            value += got_p[i, k]
        probe_grad[k, :, mine, :] = value * scale[None]
    for i in range(1, ns):
        peer = lax.rem(scan + i, ns)
        rows = probe_grad.at[:, :, mine, :]
        last.append(push(rows, rows, g_sems, i - 1, "scan", peer))
    for copy in object_copies:
        copy.wait()
    for c in range(2):
        value = placed[scan, c]
        for i in range(ns - 1):
            value += got_o[i, c]
        grad[c] = value / denom[...]
    for copy in last:
        copy.wait()


def second(ns, nt, placed, denom, part, weight_part):
    modes, _, part_rows, edge = part.shape
    own_modes = modes // nt
    block = placed.shape[1:]
    vmem = pl.BlockSpec(memory_space=pltpu.VMEM)
    dma = pltpu.SemaphoreType.DMA
    return pl.pallas_call(
        functools.partial(second_kernel, ns, nt, own_modes, part_rows),
        out_shape=(
            jax.ShapeDtypeStruct(block, F32),
            jax.ShapeDtypeStruct((own_modes, 2, edge, edge), F32),
        ),
        in_specs=[vmem] * 4,
        out_specs=(vmem,) * 2,
        scratch_shapes=[
            pltpu.VMEM((ns - 1,) + block, F32),
            pltpu.VMEM((nt - 1, own_modes, 2, part_rows, edge), F32),
            pltpu.VMEM((nt - 1, part_rows, edge), F32),
            dma((2, ns - 1)),
            dma((2, nt - 1)),
            dma((2, nt - 1)),
            dma((2, ns - 1)),
        ],
        compiler_params=pltpu.CompilerParams(
            collective_id=1, has_side_effects=True, vmem_limit_bytes=40 * 2**20
        ),
    )(placed, denom, part, weight_part)


def placement(start, offset, size, edge):
    at = start[:, None, None] + lax.broadcasted_iota(jnp.int32, (1, edge, size), 1)
    here = offset + lax.broadcasted_iota(jnp.int32, (1, edge, size), 2)
    return (at == here).astype(BF16)


def split_outside(x):
    high = lax.reduce_precision(x, 8, 7)
    return jnp.stack([high, x - high]).astype(BF16)


def place_exact(images, row_hot, col_hot):
    both = split_outside(images)
    cols = jnp.einsum("hpcab,pbj->hpcaj", both, col_hot, preferred_element_type=F32)
    cols = cols[0] + cols[1]
    both = split_outside(cols)
    out = jnp.einsum("pai,hpcaj->hcij", row_hot, both, preferred_element_type=F32)
    return out[0] + out[1]


def body(object_field, probe, measured, positions):
    strip_rows = object_field.shape[1]
    tile_cols = object_field.shape[2]
    pattern_count = measured.shape[0]
    edge_len = measured.shape[1]
    scan_count = lax.axis_size("scan")
    tile_count = lax.axis_size("tile")
    scan_index = lax.axis_index("scan")
    tile_index = lax.axis_index("tile")
    total_rows = strip_rows * scan_count
    grid_pos = positions.reshape(scan_count, tile_count, pattern_count, 2)
    row_pos = lax.dynamic_index_in_dim(grid_pos, scan_index, axis=0, keepdims=False)
    row_pos = row_pos.reshape(tile_count, 2)
    tile_left = tile_index * tile_cols
    patch, denom = cut(scan_count, tile_count, positions, object_field, probe)

    numers, part, weight_part = first(scan_count, tile_count, patch, probe, measured[0])
    row_hot = placement(row_pos[:, 0], 0, total_rows, edge_len)
    col_hot = placement(row_pos[:, 1], tile_left, tile_cols, edge_len)
    placed = place_exact(numers, row_hot, col_hot)
    placed = placed.reshape(2, scan_count, strip_rows, tile_cols).transpose(1, 0, 2, 3)
    object_gradient, probe_gradient = second(
        scan_count, tile_count, placed, denom, part, weight_part
    )
    return (object_gradient, probe_gradient)


def solution(mesh):
    return jax.shard_map(
        body,
        mesh=mesh,
        in_specs=(
            P(None, ("groups", "scan"), "tile"),
            P("groups", None, None, None),
            P(("groups", "scan", "tile"), None, None),
            P("groups", None),
        ),
        out_specs=(P(None, ("groups", "scan"), "tile"), P(("groups", "tile"), None, None, None)),
        check_vma=False,
    )
```

```python
import functools
import math

import jax
import jax.numpy as jnp
import numpy as np
from jax import lax
from jax.experimental import pallas as pl
from jax.experimental.pallas import tpu as pltpu
from jax.sharding import PartitionSpec as P

F32 = jnp.float32
BF16 = jnp.bfloat16


def dft_blocks(length):
    steps = np.arange(length)
    angle = (steps[:, None] * steps[None, :] % length) * (2.0 * math.pi / length)
    factor = 1.0 / math.sqrt(length)
    cos = np.cos(angle) * factor
    sin = -np.sin(angle) * factor
    fwd = np.block([[cos, sin], [-sin, cos]]).astype(np.float32)
    inv = np.block([[cos, -sin], [sin, cos]]).astype(np.float32)
    tables = []
    for table in (fwd, inv):
        high = table.astype(jnp.bfloat16)
        low = (table - high.astype(np.float32)).astype(jnp.bfloat16)
        tables += [high, low]
    return np.stack(tables)


def split(x):
    high = x.astype(BF16)
    return high, (x - high.astype(F32)).astype(BF16)


def dot(a, b):
    return jnp.dot(a, b, preferred_element_type=F32)


def wave_steps(edge, modes, patch, probe, measured, tables, numer, probe_numer, far, model, done):
    fwd_h, fwd_l, inv_h, inv_l = 0, 1, 2, 3

    def right(x, high_at, low_at):
        high, low = split(x)
        return dot(high, tables[high_at]) + dot(high, tables[low_at]) + dot(low, tables[high_at])

    def left(x, high_at, low_at):
        high, low = split(x)
        return dot(tables[high_at], high) + dot(tables[low_at], high) + dot(tables[high_at], low)

    def rows(x):
        return jnp.concatenate([x[:, :edge], x[:, edge:]], axis=0)

    model[...] = jnp.zeros_like(model)
    numer[...] = jnp.zeros_like(numer)

    def forward(k, carry):
        pr, pi = probe[k, 0], probe[k, 1]
        qr, qi = patch[0], patch[1]
        wave = jnp.concatenate([pr * qr - pi * qi, pr * qi + pi * qr], axis=1)
        out = left(rows(right(wave, fwd_h, fwd_l)), inv_h, inv_l)
        fr, fi = out[:edge], out[edge:]
        far[k, 0] = fr
        far[k, 1] = fi
        model[...] += fr * fr + fi * fi
        return carry

    lax.fori_loop(0, modes, forward, 0)
    model[...] = 2.0 * (model[...] - measured[...])

    def backward(k, carry):
        weight = model[...]
        wave = jnp.concatenate([weight * far[k, 0], weight * far[k, 1]], axis=1)
        out = left(rows(right(wave, inv_h, inv_l)), fwd_h, fwd_l)
        br, bi = out[:edge], out[edge:]
        pr, pi = probe[k, 0], probe[k, 1]
        qr, qi = patch[0], patch[1]
        numer[0] += pr * br + pi * bi
        numer[1] += pr * bi - pi * br
        probe_numer[k, 0] = qr * br + qi * bi
        probe_numer[k, 1] = qr * bi - qi * br
        done(k)
        return carry

    lax.fori_loop(0, modes, backward, 0)


MESH = pl.DeviceIdType.MESH


def greet(counts):
    barrier = pltpu.get_barrier_semaphore()
    total = 0
    for axis, count in counts:
        me = lax.axis_index(axis)
        for i in range(1, count):
            pl.semaphore_signal(
                barrier, inc=1, device_id={axis: lax.rem(me + i, count)}, device_id_type=MESH
            )
            total += 1
    pl.semaphore_wait(barrier, total)


def push(src, dst, sems, at, axis, peer):
    copy = pltpu.make_async_remote_copy(
        src_ref=src,
        dst_ref=dst,
        send_sem=sems.at[0, at],
        recv_sem=sems.at[1, at],
        device_id={axis: peer},
        device_id_type=MESH,
    )
    copy.start()
    return copy


def relay(nt, slots, sems):
    tile = lax.axis_index("tile")

    def copy(slot, way, hop, peer, c):
        at = jnp.clip(slot, 0, nt - 1)
        return pltpu.make_async_remote_copy(
            src_ref=slots.at[at, c],
            dst_ref=slots.at[at, c],
            send_sem=sems.at[0, way, hop, c],
            recv_sem=sems.at[1, way, hop, c],
            device_id={"tile": jnp.clip(peer, 0, nt - 1)},
            device_id_type=MESH,
        )

    def send_up(hop, c, act):
        pl.when(jnp.logical_and(tile + 1 < nt, tile - hop >= 0))(
            lambda: act(copy(tile - hop, 0, hop, tile + 1, c))
        )

    def send_down(hop, c, act):
        pl.when(jnp.logical_and(tile - 1 >= 0, tile + hop < nt))(
            lambda: act(copy(tile + hop, 1, hop, tile - 1, c))
        )

    def start(hop):
        for c in range(2):
            send_up(hop, c, lambda d: d.start())
            send_down(hop, c, lambda d: d.start())

    def finish(hop):
        for c in range(2):
            send_up(hop, c, lambda d: d.wait_send())
            send_down(hop, c, lambda d: d.wait_send())

    def receive(hop):
        for c in range(2):
            pl.when(tile - 1 - hop >= 0)(
                lambda: copy(tile - 1 - hop, 0, hop, tile - 1, c).wait_recv()
            )
            if hop + 1 < nt - 1:
                send_up(hop + 1, c, lambda d: d.start())
            pl.when(tile + 1 + hop < nt)(
                lambda: copy(tile + 1 + hop, 1, hop, tile + 1, c).wait_recv()
            )
            if hop + 1 < nt - 1:
                send_down(hop + 1, c, lambda d: d.start())

    return start, receive, finish


def hot(shape, row_start, col_start):
    rows = row_start + lax.broadcasted_iota(jnp.int32, shape, 0)
    cols = col_start + lax.broadcasted_iota(jnp.int32, shape, 1)
    return (rows == cols).astype(F32).astype(BF16)


def cut_kernel(
    ns, nt, positions, tile_ref, probe, patch, denom, tiles, pieces, got, power, t_sems, s_sems
):
    scan, tile = lax.axis_index("scan"), lax.axis_index("tile")
    strip_rows, tile_cols = tile_ref.shape[1:]
    edge = patch.shape[1]
    modes = probe.shape[0]
    greet((("scan", ns), ("tile", nt)))
    tiles[tile] = tile_ref[...]
    start, receive, finish = relay(nt, tiles, t_sems)
    start(0)
    pieces[...] = jnp.zeros_like(pieces)

    def cut(slot):
        high, low = split(tiles[slot].reshape(2 * strip_rows, tile_cols))

        def one(i, carry):
            col_at = positions[i * nt + tile, 1]
            pick = hot((tile_cols, edge), slot * tile_cols, col_at)
            pieces[i] += (dot(high, pick) + dot(low, pick)).reshape(2, strip_rows, edge)
            return carry

        lax.fori_loop(0, ns, one, 0)

    cut(tile)
    power[...] = jnp.zeros_like(power)

    def add_power(k, carry):
        power[...] += probe[k, 0] * probe[k, 0] + probe[k, 1] * probe[k, 1]
        return carry

    lax.fori_loop(0, modes, add_power, 0)
    denom[...] = jnp.zeros_like(denom)

    def add_weight(j, carry):
        row_pick = hot((strip_rows, edge), scan * strip_rows, positions[j, 0])
        col_pick = hot((edge, tile_cols), positions[j, 1], tile * tile_cols)
        high, low = split(power[...])
        rows = dot(row_pick, high) + dot(row_pick, low)
        high, low = split(rows)
        denom[...] += dot(high, col_pick) + dot(low, col_pick)
        return carry

    lax.fori_loop(0, positions.shape[0], add_weight, 0)
    denom[...] = jnp.maximum(denom[...], 1.0)
    for hop in range(nt - 1):
        receive(hop)
        pl.when(tile - 1 - hop >= 0)(lambda: cut(jnp.maximum(tile - 1 - hop, 0)))
        pl.when(tile + 1 + hop < nt)(lambda: cut(jnp.minimum(tile + 1 + hop, nt - 1)))
    copies = []
    for i in range(1, ns):
        peer = lax.rem(scan + i, ns)
        copies.append(push(pieces.at[peer], got.at[i - 1], s_sems, i - 1, "scan", peer))
    row_at = positions[scan * nt + tile, 0]

    def add_rows(piece, source):
        pick = hot((edge, strip_rows), row_at, source * strip_rows)
        out = []
        for c in range(2):
            high, low = split(piece[c])
            out.append(dot(pick, high) + dot(pick, low))
        return jnp.stack(out)

    patch[...] = add_rows(pieces[scan], scan)
    for copy in copies:
        copy.wait()
    for i in range(1, ns):
        patch[...] += add_rows(got[i - 1], lax.rem(scan + ns - i, ns))
    for hop in range(nt - 1):
        finish(hop)


def cut(ns, nt, positions, tile_block, probe):
    _, strip_rows, tile_cols = tile_block.shape
    edge = probe.shape[2]
    vmem = pl.BlockSpec(memory_space=pltpu.VMEM)
    dma = pltpu.SemaphoreType.DMA
    return pl.pallas_call(
        functools.partial(cut_kernel, ns, nt),
        out_shape=(
            jax.ShapeDtypeStruct((2, edge, edge), F32),
            jax.ShapeDtypeStruct((strip_rows, tile_cols), F32),
        ),
        in_specs=[pl.BlockSpec(memory_space=pltpu.SMEM), vmem, vmem],
        out_specs=(vmem,) * 2,
        scratch_shapes=[
            pltpu.VMEM((nt, 2, strip_rows, tile_cols), F32),
            pltpu.VMEM((ns, 2, strip_rows, edge), F32),
            pltpu.VMEM((ns - 1, 2, strip_rows, edge), F32),
            pltpu.VMEM((edge, edge), F32),
            dma((2, 2, nt - 1, 2)),
            dma((2, ns - 1)),
        ],
        compiler_params=pltpu.CompilerParams(
            collective_id=2, has_side_effects=True, vmem_limit_bytes=40 * 2**20
        ),
    )(positions, tile_block, probe)


def row_block(ns, scan, part_rows):
    at = lax.rem(scan, 2) * (ns // 2) + scan // 2
    return pl.ds(pl.multiple_of(at * part_rows, part_rows), part_rows)


def first_kernel(
    ns, nt, modes, part_rows, patch, probe, measured, tables, numers, part, weight_part,
    far, model, numer, probe_numer, weight, got_c, half, got_x, got_w,
    z_sems, c_sems, x_sems, w_sems,
):
    scan, tile = lax.axis_index("scan"), lax.axis_index("tile")
    core, column, nx = lax.rem(scan, 2), scan // 2, ns // 2
    edge = patch.shape[1]
    half_rows = nx * part_rows
    greet((("scan", ns), ("tile", nt)))
    weight[...] = patch[0] * patch[0] + patch[1] * patch[1]
    weights = []
    for i in range(1, ns):
        peer = lax.rem(scan + i, ns)
        rows = weight.at[row_block(ns, peer, part_rows), :]
        weights.append(push(rows, got_w.at[i - 1], w_sems, i - 1, "scan", peer))

    def to_core(k):
        rows = pl.ds(pl.multiple_of((1 - core) * half_rows, half_rows), half_rows)
        return pltpu.make_async_remote_copy(
            src_ref=probe_numer.at[k, :, rows, :],
            dst_ref=got_c.at[k],
            send_sem=c_sems.at[0, k],
            recv_sem=c_sems.at[1, k],
            device_id={"scan": scan + 1 - 2 * core},
            device_id_type=MESH,
        )

    def to_chip(k, i):
        peer = lax.rem(column + i, nx)
        rows = pl.ds(pl.multiple_of(peer * part_rows, part_rows), part_rows)
        return pltpu.make_async_remote_copy(
            src_ref=half.at[k, :, rows, :],
            dst_ref=got_x.at[i - 1, k],
            send_sem=x_sems.at[0, i - 1, k],
            recv_sem=x_sems.at[1, i - 1, k],
            device_id={"scan": peer * 2 + core},
            device_id_type=MESH,
        )

    def pass_on(k):
        to_core(k).wait()
        rows = pl.ds(pl.multiple_of(core * half_rows, half_rows), half_rows)
        half[k] = probe_numer[k, :, rows, :] + got_c[k]
        for i in range(1, nx):
            to_chip(k, i).start()

    def done(k):
        to_core(k).start()
        pl.when(k >= 2)(lambda: pass_on(jnp.maximum(k - 2, 0)))

    wave_steps(edge, modes, patch, probe, measured, tables, numer, probe_numer, far, model, done)
    numers[tile] = numer[...]
    start, receive, finish = relay(nt, numers, z_sems)
    start(0)
    for k in range(max(modes - 2, 0), modes):
        pass_on(k)
    for hop in range(nt - 1):
        receive(hop)
    for copy in weights:
        copy.wait()
    total = weight[row_block(ns, scan, part_rows), :]
    for i in range(ns - 1):
        total += got_w[i]
    weight_part[...] = total

    def add(k, carry):
        rows = pl.ds(pl.multiple_of(column * part_rows, part_rows), part_rows)
        for i in range(1, nx):
            to_chip(k, i).wait()
        value = half[k, :, rows, :]
        for i in range(nx - 1):
            value += got_x[i, k]
        part[k] = value
        return carry

    lax.fori_loop(0, modes, add, 0)
    for hop in range(nt - 1):
        finish(hop)


def first(ns, nt, patch, probe, measured):
    modes, _, edge, _ = probe.shape
    part_rows = edge // ns
    nx = ns // 2
    half_rows = nx * part_rows
    vmem = pl.BlockSpec(memory_space=pltpu.VMEM)
    dma = pltpu.SemaphoreType.DMA
    return pl.pallas_call(
        functools.partial(first_kernel, ns, nt, modes, part_rows),
        out_shape=(
            jax.ShapeDtypeStruct((nt, 2, edge, edge), F32),
            jax.ShapeDtypeStruct((modes, 2, part_rows, edge), F32),
            jax.ShapeDtypeStruct((part_rows, edge), F32),
        ),
        in_specs=[vmem] * 4,
        out_specs=(vmem,) * 3,
        scratch_shapes=[
            pltpu.VMEM((modes, 2, edge, edge), F32),
            pltpu.VMEM((edge, edge), F32),
            pltpu.VMEM((2, edge, edge), F32),
            pltpu.VMEM((modes, 2, edge, edge), F32),
            pltpu.VMEM((edge, edge), F32),
            pltpu.VMEM((modes, 2, half_rows, edge), F32),
            pltpu.VMEM((modes, 2, half_rows, edge), F32),
            pltpu.VMEM((nx - 1, modes, 2, part_rows, edge), F32),
            pltpu.VMEM((ns - 1, part_rows, edge), F32),
            dma((2, 2, nt - 1, 2)),
            dma((2, modes)),
            dma((2, nx - 1, modes)),
            dma((2, ns - 1)),
        ],
        compiler_params=pltpu.CompilerParams(
            collective_id=0, has_side_effects=True, vmem_limit_bytes=48 * 2**20
        ),
    )(patch, probe, measured, jnp.asarray(dft_blocks(edge)))


def second_kernel(
    ns, nt, own_modes, part_rows, positions, numers, denom, part, weight_part, grad, probe_grad, placed, cols_h, cols_l, got_o, got_p, got_w, o_sems, p_sems, w_sems, g_sems
):
    scan, tile = lax.axis_index("scan"), lax.axis_index("tile")
    greet((("scan", ns), ("tile", nt)))
    probe_copies, object_copies, last = [], [], []
    for i in range(1, nt):
        peer = lax.rem(tile + i, nt)
        span = pl.ds(peer * own_modes, own_modes)
        probe_copies.append(push(weight_part, got_w.at[i - 1], w_sems, i - 1, "tile", peer))
        probe_copies.append(push(part.at[span], got_p.at[i - 1], p_sems, i - 1, "tile", peer))
    strip_rows, tile_cols = denom.shape
    edge = numers.shape[2]

    def columns(o, carry):
        pick = hot((edge, tile_cols), positions[scan * nt + o, 1], tile * tile_cols)
        high, low = split(numers[o].reshape(2 * edge, edge))
        high, low = split((dot(high, pick) + dot(low, pick)).reshape(2, edge, tile_cols))
        cols_h[o] = high
        cols_l[o] = low
        return carry

    lax.fori_loop(0, nt, columns, 0)

    def place(dest):
        placed[dest] = jnp.zeros((2, strip_rows, tile_cols), F32)

        def one(o, carry):
            pick = hot((strip_rows, edge), dest * strip_rows, positions[scan * nt + o, 0])
            for c in range(2):
                placed[dest, c] += dot(pick, cols_h[o, c]) + dot(pick, cols_l[o, c])
            return carry

        lax.fori_loop(0, nt, one, 0)

    for i in range(1, ns):
        peer = lax.rem(scan + i, ns)
        place(peer)
        object_copies.append(push(placed.at[peer], got_o.at[i - 1], o_sems, i - 1, "scan", peer))
    place(scan)
    for copy in probe_copies:
        copy.wait()
    total = weight_part[...]
    for i in range(nt - 1):
        total += got_w[i]
    scale = 1.0 / (total + 1e-05)
    mine = row_block(ns, scan, part_rows)
    for k in range(own_modes):
        value = part[tile * own_modes + k]
        for i in range(nt - 1):
            value += got_p[i, k]
        probe_grad[k, :, mine, :] = value * scale[None]
    for i in range(1, ns):
        peer = lax.rem(scan + i, ns)
        rows = probe_grad.at[:, :, mine, :]
        last.append(push(rows, rows, g_sems, i - 1, "scan", peer))
    for copy in object_copies:
        copy.wait()
    for c in range(2):
        value = placed[scan, c]
        for i in range(ns - 1):
            value += got_o[i, c]
        grad[c] = value / denom[...]
    for copy in last:
        copy.wait()


def second(ns, nt, positions, numers, denom, part, weight_part):
    modes, _, part_rows, edge = part.shape
    own_modes = modes // nt
    block = (2,) + denom.shape
    vmem = pl.BlockSpec(memory_space=pltpu.VMEM)
    dma = pltpu.SemaphoreType.DMA
    return pl.pallas_call(
        functools.partial(second_kernel, ns, nt, own_modes, part_rows),
        out_shape=(
            jax.ShapeDtypeStruct(block, F32),
            jax.ShapeDtypeStruct((own_modes, 2, edge, edge), F32),
        ),
        in_specs=[pl.BlockSpec(memory_space=pltpu.SMEM)] + [vmem] * 4,
        out_specs=(vmem,) * 2,
        scratch_shapes=[
            pltpu.VMEM((ns,) + block, F32),
            pltpu.VMEM((nt, 2, edge, denom.shape[1]), BF16),
            pltpu.VMEM((nt, 2, edge, denom.shape[1]), BF16),
            pltpu.VMEM((ns - 1,) + block, F32),
            pltpu.VMEM((nt - 1, own_modes, 2, part_rows, edge), F32),
            pltpu.VMEM((nt - 1, part_rows, edge), F32),
            dma((2, ns - 1)),
            dma((2, nt - 1)),
            dma((2, nt - 1)),
            dma((2, ns - 1)),
        ],
        compiler_params=pltpu.CompilerParams(
            collective_id=1, has_side_effects=True, vmem_limit_bytes=40 * 2**20
        ),
    )(positions, numers, denom, part, weight_part)


def body(object_field, probe, measured, positions):
    scan_count = lax.axis_size("scan")
    tile_count = lax.axis_size("tile")
    patch, denom = cut(scan_count, tile_count, positions, object_field, probe)

    numers, part, weight_part = first(scan_count, tile_count, patch, probe, measured[0])
    object_gradient, probe_gradient = second(
        scan_count, tile_count, positions, numers, denom, part, weight_part
    )
    return (object_gradient, probe_gradient)


def solution(mesh):
    return jax.shard_map(
        body,
        mesh=mesh,
        in_specs=(
            P(None, ("groups", "scan"), "tile"),
            P("groups", None, None, None),
            P(("groups", "scan", "tile"), None, None),
            P("groups", None),
        ),
        out_specs=(P(None, ("groups", "scan"), "tile"), P(("groups", "tile"), None, None, None)),
        check_vma=False,
    )
```

```python
import functools
import math

import jax
import jax.numpy as jnp
import numpy as np
from jax import lax
from jax.experimental import pallas as pl
from jax.experimental.pallas import tpu as pltpu
from jax.sharding import PartitionSpec as P

F32 = jnp.float32
BF16 = jnp.bfloat16


def dft_blocks(length):
    steps = np.arange(length)
    angle = (steps[:, None] * steps[None, :] % length) * (2.0 * math.pi / length)
    factor = 1.0 / math.sqrt(length)
    cos = np.cos(angle) * factor
    sin = -np.sin(angle) * factor
    fwd = np.block([[cos, sin], [-sin, cos]]).astype(np.float32)
    inv = np.block([[cos, -sin], [sin, cos]]).astype(np.float32)
    tables = []
    for table in (fwd, inv):
        high = table.astype(jnp.bfloat16)
        low = (table - high.astype(np.float32)).astype(jnp.bfloat16)
        tables += [high, low]
    return np.stack(tables)


def split(x):
    high = x.astype(BF16)
    return high, (x - high.astype(F32)).astype(BF16)


def dot(a, b):
    return jnp.dot(a, b, preferred_element_type=F32)


def wave_steps(edge, modes, patch, probe, measured, tables, numer, probe_numer, far, model, done):
    fwd_h, fwd_l, inv_h, inv_l = 0, 1, 2, 3

    def right(x, high_at, low_at):
        high, low = split(x)
        return dot(high, tables[high_at]) + dot(high, tables[low_at]) + dot(low, tables[high_at])

    def left(x, high_at, low_at):
        high, low = split(x)
        return dot(tables[high_at], high) + dot(tables[low_at], high) + dot(tables[high_at], low)

    def rows(x):
        return jnp.concatenate([x[:, :edge], x[:, edge:]], axis=0)

    model[...] = jnp.zeros_like(model)
    numer[...] = jnp.zeros_like(numer)

    def forward(k, carry):
        pr, pi = probe[k, 0], probe[k, 1]
        qr, qi = patch[0], patch[1]
        wave = jnp.concatenate([pr * qr - pi * qi, pr * qi + pi * qr], axis=1)
        out = left(rows(right(wave, fwd_h, fwd_l)), inv_h, inv_l)
        fr, fi = out[:edge], out[edge:]
        far[k, 0] = fr
        far[k, 1] = fi
        model[...] += fr * fr + fi * fi
        return carry

    lax.fori_loop(0, modes, forward, 0)
    model[...] = 2.0 * (model[...] - measured[...])

    def backward(k, carry):
        weight = model[...]
        wave = jnp.concatenate([weight * far[k, 0], weight * far[k, 1]], axis=1)
        out = left(rows(right(wave, inv_h, inv_l)), fwd_h, fwd_l)
        br, bi = out[:edge], out[edge:]
        pr, pi = probe[k, 0], probe[k, 1]
        qr, qi = patch[0], patch[1]
        numer[0] += pr * br + pi * bi
        numer[1] += pr * bi - pi * br
        probe_numer[k, 0] = qr * br + qi * bi
        probe_numer[k, 1] = qr * bi - qi * br
        done(k)
        return carry

    lax.fori_loop(0, modes, backward, 0)


MESH = pl.DeviceIdType.MESH


def greet(counts):
    barrier = pltpu.get_barrier_semaphore()
    total = 0
    for axis, count in counts:
        me = lax.axis_index(axis)
        for i in range(1, count):
            pl.semaphore_signal(
                barrier, inc=1, device_id={axis: lax.rem(me + i, count)}, device_id_type=MESH
            )
            total += 1
    pl.semaphore_wait(barrier, total)


def push(src, dst, sems, at, axis, peer):
    copy = pltpu.make_async_remote_copy(
        src_ref=src,
        dst_ref=dst,
        send_sem=sems.at[0, at],
        recv_sem=sems.at[1, at],
        device_id={axis: peer},
        device_id_type=MESH,
    )
    copy.start()
    return copy


def relay(nt, slots, sems):
    tile = lax.axis_index("tile")

    def copy(slot, way, hop, peer, c):
        at = jnp.clip(slot, 0, nt - 1)
        return pltpu.make_async_remote_copy(
            src_ref=slots.at[at, c],
            dst_ref=slots.at[at, c],
            send_sem=sems.at[0, way, hop, c],
            recv_sem=sems.at[1, way, hop, c],
            device_id={"tile": jnp.clip(peer, 0, nt - 1)},
            device_id_type=MESH,
        )

    def send_up(hop, c, act):
        pl.when(jnp.logical_and(tile + 1 < nt, tile - hop >= 0))(
            lambda: act(copy(tile - hop, 0, hop, tile + 1, c))
        )

    def send_down(hop, c, act):
        pl.when(jnp.logical_and(tile - 1 >= 0, tile + hop < nt))(
            lambda: act(copy(tile + hop, 1, hop, tile - 1, c))
        )

    def start(hop):
        for c in range(2):
            send_up(hop, c, lambda d: d.start())
            send_down(hop, c, lambda d: d.start())

    def finish(hop):
        for c in range(2):
            send_up(hop, c, lambda d: d.wait_send())
            send_down(hop, c, lambda d: d.wait_send())

    def receive(hop):
        for c in range(2):
            pl.when(tile - 1 - hop >= 0)(
                lambda: copy(tile - 1 - hop, 0, hop, tile - 1, c).wait_recv()
            )
            if hop + 1 < nt - 1:
                send_up(hop + 1, c, lambda d: d.start())
            pl.when(tile + 1 + hop < nt)(
                lambda: copy(tile + 1 + hop, 1, hop, tile + 1, c).wait_recv()
            )
            if hop + 1 < nt - 1:
                send_down(hop + 1, c, lambda d: d.start())

    return start, receive, finish


def hot(shape, row_start, col_start):
    rows = row_start + lax.broadcasted_iota(jnp.int32, shape, 0)
    cols = col_start + lax.broadcasted_iota(jnp.int32, shape, 1)
    return (rows == cols).astype(F32).astype(BF16)


def cut_kernel(
    ns, nt, positions, tile_ref, probe, patch, denom, tiles, pieces, got, power, t_sems, s_sems
):
    scan, tile = lax.axis_index("scan"), lax.axis_index("tile")
    strip_rows, tile_cols = tile_ref.shape[1:]
    edge = patch.shape[1]
    modes = probe.shape[0]
    greet((("scan", ns), ("tile", nt)))
    tiles[tile] = tile_ref[...]
    start, receive, finish = relay(nt, tiles, t_sems)
    start(0)
    pieces[...] = jnp.zeros_like(pieces)

    def cut(slot):
        high, low = split(tiles[slot].reshape(2 * strip_rows, tile_cols))

        def one(i, carry):
            col_at = positions[i * nt + tile, 1]
            pick = hot((tile_cols, edge), slot * tile_cols, col_at)
            pieces[i] += (dot(high, pick) + dot(low, pick)).reshape(2, strip_rows, edge)
            return carry

        lax.fori_loop(0, ns, one, 0)

    cut(tile)
    power[...] = jnp.zeros_like(power)

    def add_power(k, carry):
        power[...] += probe[k, 0] * probe[k, 0] + probe[k, 1] * probe[k, 1]
        return carry

    lax.fori_loop(0, modes, add_power, 0)
    denom[...] = jnp.zeros_like(denom)

    def add_weight(j, carry):
        row_pick = hot((strip_rows, edge), scan * strip_rows, positions[j, 0])
        col_pick = hot((edge, tile_cols), positions[j, 1], tile * tile_cols)
        high, low = split(power[...])
        rows = dot(row_pick, high) + dot(row_pick, low)
        high, low = split(rows)
        denom[...] += dot(high, col_pick) + dot(low, col_pick)
        return carry

    lax.fori_loop(0, positions.shape[0], add_weight, 0)
    denom[...] = jnp.maximum(denom[...], 1.0)
    for hop in range(nt - 1):
        receive(hop)
        pl.when(tile - 1 - hop >= 0)(lambda: cut(jnp.maximum(tile - 1 - hop, 0)))
        pl.when(tile + 1 + hop < nt)(lambda: cut(jnp.minimum(tile + 1 + hop, nt - 1)))
    copies = []
    for i in range(1, ns):
        peer = lax.rem(scan + i, ns)
        copies.append(push(pieces.at[peer], got.at[i - 1], s_sems, i - 1, "scan", peer))
    row_at = positions[scan * nt + tile, 0]

    def add_rows(piece, source):
        pick = hot((edge, strip_rows), row_at, source * strip_rows)
        out = []
        for c in range(2):
            high, low = split(piece[c])
            out.append(dot(pick, high) + dot(pick, low))
        return jnp.stack(out)

    patch[...] = add_rows(pieces[scan], scan)
    for copy in copies:
        copy.wait()
    for i in range(1, ns):
        patch[...] += add_rows(got[i - 1], lax.rem(scan + ns - i, ns))
    for hop in range(nt - 1):
        finish(hop)


def cut(ns, nt, positions, tile_block, probe):
    _, strip_rows, tile_cols = tile_block.shape
    edge = probe.shape[2]
    vmem = pl.BlockSpec(memory_space=pltpu.VMEM)
    dma = pltpu.SemaphoreType.DMA
    return pl.pallas_call(
        functools.partial(cut_kernel, ns, nt),
        out_shape=(
            jax.ShapeDtypeStruct((2, edge, edge), F32),
            jax.ShapeDtypeStruct((strip_rows, tile_cols), F32),
        ),
        in_specs=[pl.BlockSpec(memory_space=pltpu.SMEM), vmem, vmem],
        out_specs=(vmem,) * 2,
        scratch_shapes=[
            pltpu.VMEM((nt, 2, strip_rows, tile_cols), F32),
            pltpu.VMEM((ns, 2, strip_rows, edge), F32),
            pltpu.VMEM((ns - 1, 2, strip_rows, edge), F32),
            pltpu.VMEM((edge, edge), F32),
            dma((2, 2, nt - 1, 2)),
            dma((2, ns - 1)),
        ],
        compiler_params=pltpu.CompilerParams(
            collective_id=2, has_side_effects=True, vmem_limit_bytes=40 * 2**20
        ),
    )(positions, tile_block, probe)


def row_block(ns, scan, part_rows):
    at = lax.rem(scan, 2) * (ns // 2) + scan // 2
    return pl.ds(pl.multiple_of(at * part_rows, part_rows), part_rows)


def first_kernel(
    ns, nt, modes, part_rows, patch, probe, measured, tables, numers, part, weight_part,
    far, model, numer, probe_numer, weight, got_c, half, got_x, got_w,
    z_sems, c_sems, x_sems, w_sems,
):
    scan, tile = lax.axis_index("scan"), lax.axis_index("tile")
    core, column, nx = lax.rem(scan, 2), scan // 2, ns // 2
    edge = patch.shape[1]
    half_rows = nx * part_rows
    greet((("scan", ns), ("tile", nt)))
    weight[...] = patch[0] * patch[0] + patch[1] * patch[1]
    weights = []
    for i in range(1, ns):
        peer = lax.rem(scan + i, ns)
        rows = weight.at[row_block(ns, peer, part_rows), :]
        weights.append(push(rows, got_w.at[i - 1], w_sems, i - 1, "scan", peer))

    def to_core(k):
        rows = pl.ds(pl.multiple_of((1 - core) * half_rows, half_rows), half_rows)
        return pltpu.make_async_remote_copy(
            src_ref=probe_numer.at[k, :, rows, :],
            dst_ref=got_c.at[k],
            send_sem=c_sems.at[0, k],
            recv_sem=c_sems.at[1, k],
            device_id={"scan": scan + 1 - 2 * core},
            device_id_type=MESH,
        )

    def to_chip(k, i):
        peer = lax.rem(column + i, nx)
        rows = pl.ds(pl.multiple_of(peer * part_rows, part_rows), part_rows)
        return pltpu.make_async_remote_copy(
            src_ref=half.at[k, :, rows, :],
            dst_ref=got_x.at[i - 1, k],
            send_sem=x_sems.at[0, i - 1, k],
            recv_sem=x_sems.at[1, i - 1, k],
            device_id={"scan": peer * 2 + core},
            device_id_type=MESH,
        )

    def pass_on(k):
        to_core(k).wait()
        rows = pl.ds(pl.multiple_of(core * half_rows, half_rows), half_rows)
        half[k] = probe_numer[k, :, rows, :] + got_c[k]
        for i in range(1, nx):
            to_chip(k, i).start()

    def done(k):
        to_core(k).start()
        pl.when(k >= 2)(lambda: pass_on(jnp.maximum(k - 2, 0)))

    wave_steps(edge, modes, patch, probe, measured, tables, numer, probe_numer, far, model, done)
    numers[tile] = numer[...]
    start, receive, finish = relay(nt, numers, z_sems)
    start(0)
    for k in range(max(modes - 2, 0), modes):
        pass_on(k)
    for hop in range(nt - 1):
        receive(hop)
    for copy in weights:
        copy.wait()
    total = weight[row_block(ns, scan, part_rows), :]
    for i in range(ns - 1):
        total += got_w[i]
    weight_part[...] = total

    def add(k, carry):
        rows = pl.ds(pl.multiple_of(column * part_rows, part_rows), part_rows)
        for i in range(1, nx):
            to_chip(k, i).wait()
        value = half[k, :, rows, :]
        for i in range(nx - 1):
            value += got_x[i, k]
        part[k] = value
        return carry

    lax.fori_loop(0, modes, add, 0)
    for hop in range(nt - 1):
        finish(hop)


def first(ns, nt, patch, probe, measured):
    modes, _, edge, _ = probe.shape
    part_rows = edge // ns
    nx = ns // 2
    half_rows = nx * part_rows
    vmem = pl.BlockSpec(memory_space=pltpu.VMEM)
    dma = pltpu.SemaphoreType.DMA
    return pl.pallas_call(
        functools.partial(first_kernel, ns, nt, modes, part_rows),
        out_shape=(
            jax.ShapeDtypeStruct((nt, 2, edge, edge), F32),
            jax.ShapeDtypeStruct((modes, 2, part_rows, edge), F32),
            jax.ShapeDtypeStruct((part_rows, edge), F32),
        ),
        in_specs=[vmem] * 4,
        out_specs=(vmem,) * 3,
        scratch_shapes=[
            pltpu.VMEM((modes, 2, edge, edge), F32),
            pltpu.VMEM((edge, edge), F32),
            pltpu.VMEM((2, edge, edge), F32),
            pltpu.VMEM((modes, 2, edge, edge), F32),
            pltpu.VMEM((edge, edge), F32),
            pltpu.VMEM((modes, 2, half_rows, edge), F32),
            pltpu.VMEM((modes, 2, half_rows, edge), F32),
            pltpu.VMEM((nx - 1, modes, 2, part_rows, edge), F32),
            pltpu.VMEM((ns - 1, part_rows, edge), F32),
            dma((2, 2, nt - 1, 2)),
            dma((2, modes)),
            dma((2, nx - 1, modes)),
            dma((2, ns - 1)),
        ],
        compiler_params=pltpu.CompilerParams(
            collective_id=0, has_side_effects=True, vmem_limit_bytes=48 * 2**20
        ),
    )(patch, probe, measured, jnp.asarray(dft_blocks(edge)))


def second_kernel(
    ns, nt, own_modes, part_rows, positions, numers, denom, part, weight_part, grad, probe_grad, placed, cols_h, cols_l, got_c, got_o, got_p, got_w, c_sems, o_sems, p_sems, w_sems, g_sems
):
    scan, tile = lax.axis_index("scan"), lax.axis_index("tile")
    greet((("scan", ns), ("tile", nt)))
    probe_copies, object_copies, last = [], [], []
    for i in range(1, nt):
        peer = lax.rem(tile + i, nt)
        span = pl.ds(peer * own_modes, own_modes)
        probe_copies.append(push(weight_part, got_w.at[i - 1], w_sems, i - 1, "tile", peer))
        probe_copies.append(push(part.at[span], got_p.at[i - 1], p_sems, i - 1, "tile", peer))
    strip_rows, tile_cols = denom.shape
    edge = numers.shape[2]

    def columns(o, carry):
        pick = hot((edge, tile_cols), positions[scan * nt + o, 1], tile * tile_cols)
        high, low = split(numers[o].reshape(2 * edge, edge))
        high, low = split((dot(high, pick) + dot(low, pick)).reshape(2, edge, tile_cols))
        cols_h[o] = high
        cols_l[o] = low
        return carry

    lax.fori_loop(0, nt, columns, 0)

    def place(dest):
        placed[dest] = jnp.zeros((2, strip_rows, tile_cols), F32)

        def one(o, carry):
            pick = hot((strip_rows, edge), dest * strip_rows, positions[scan * nt + o, 0])
            for c in range(2):
                placed[dest, c] += dot(pick, cols_h[o, c]) + dot(pick, cols_l[o, c])
            return carry

        lax.fori_loop(0, nt, one, 0)

    core, column, nx = lax.rem(scan, 2), scan // 2, ns // 2
    core_copies = []
    for p in range(nx):
        dest = p * 2 + 1 - core
        place(dest)
        core_copies.append(
            push(placed.at[dest], got_c.at[p], c_sems, p, "scan", scan + 1 - 2 * core)
        )
    for p in range(nx):
        place(p * 2 + core)
    for p in range(nx):
        core_copies[p].wait()
        placed[p * 2 + core] += got_c[p]
    for i in range(1, nx):
        peer = lax.rem(column + i, nx) * 2 + core
        object_copies.append(push(placed.at[peer], got_o.at[i - 1], o_sems, i - 1, "scan", peer))
    for copy in probe_copies:
        copy.wait()
    total = weight_part[...]
    for i in range(nt - 1):
        total += got_w[i]
    scale = 1.0 / (total + 1e-05)
    mine = row_block(ns, scan, part_rows)
    for k in range(own_modes):
        value = part[tile * own_modes + k]
        for i in range(nt - 1):
            value += got_p[i, k]
        probe_grad[k, :, mine, :] = value * scale[None]
    for i in range(1, ns):
        peer = lax.rem(scan + i, ns)
        rows = probe_grad.at[:, :, mine, :]
        last.append(push(rows, rows, g_sems, i - 1, "scan", peer))
    for copy in object_copies:
        copy.wait()
    for c in range(2):
        value = placed[scan, c]
        for i in range(nx - 1):
            value += got_o[i, c]
        grad[c] = value / denom[...]
    for copy in last:
        copy.wait()


def second(ns, nt, positions, numers, denom, part, weight_part):
    modes, _, part_rows, edge = part.shape
    own_modes = modes // nt
    block = (2,) + denom.shape
    vmem = pl.BlockSpec(memory_space=pltpu.VMEM)
    dma = pltpu.SemaphoreType.DMA
    return pl.pallas_call(
        functools.partial(second_kernel, ns, nt, own_modes, part_rows),
        out_shape=(
            jax.ShapeDtypeStruct(block, F32),
            jax.ShapeDtypeStruct((own_modes, 2, edge, edge), F32),
        ),
        in_specs=[pl.BlockSpec(memory_space=pltpu.SMEM)] + [vmem] * 4,
        out_specs=(vmem,) * 2,
        scratch_shapes=[
            pltpu.VMEM((ns,) + block, F32),
            pltpu.VMEM((nt, 2, edge, denom.shape[1]), BF16),
            pltpu.VMEM((nt, 2, edge, denom.shape[1]), BF16),
            pltpu.VMEM((ns // 2,) + block, F32),
            pltpu.VMEM((ns // 2 - 1,) + block, F32),
            pltpu.VMEM((nt - 1, own_modes, 2, part_rows, edge), F32),
            pltpu.VMEM((nt - 1, part_rows, edge), F32),
            dma((2, ns // 2)),
            dma((2, ns // 2 - 1)),
            dma((2, nt - 1)),
            dma((2, nt - 1)),
            dma((2, ns - 1)),
        ],
        compiler_params=pltpu.CompilerParams(
            collective_id=1, has_side_effects=True, vmem_limit_bytes=40 * 2**20
        ),
    )(positions, numers, denom, part, weight_part)


def body(object_field, probe, measured, positions):
    scan_count = lax.axis_size("scan")
    tile_count = lax.axis_size("tile")
    patch, denom = cut(scan_count, tile_count, positions, object_field, probe)

    numers, part, weight_part = first(scan_count, tile_count, patch, probe, measured[0])
    object_gradient, probe_gradient = second(
        scan_count, tile_count, positions, numers, denom, part, weight_part
    )
    return (object_gradient, probe_gradient)


def solution(mesh):
    return jax.shard_map(
        body,
        mesh=mesh,
        in_specs=(
            P(None, ("groups", "scan"), "tile"),
            P("groups", None, None, None),
            P(("groups", "scan", "tile"), None, None),
            P("groups", None),
        ),
        out_specs=(P(None, ("groups", "scan"), "tile"), P(("groups", "tile"), None, None, None)),
        check_vma=False,
    )
```
